512 devices in a mesh: mode: 32 (over y, x, core), tm: 16 (over z).
Axes of the slice: x: 4, y: 4, z: 16, core: 2. Of those that a mesh axis runs over, the one named last changes fastest.
Arguments:
- field: float32 [2, 128, 65536], P(None, 'mode', 'tm'), may hold values from -1.8 to 1.8
- beta: float32 [3, 128], P(None, 'mode'), may hold values from -1 to 1
- quartets: int32 [4, 1024], replicated, may hold values from 0 to 127
- intersections: float32 [1024], replicated, may hold values from -0.12 to 0.12
Outputs:
- field_out: float32 [2, 128, 65536], P(None, 'mode', 'tm')
- errors: float32 [2, 128], P(None, 'mode')
The draws below stay inside these ranges and needn't reach their ends.
All inputs are finite; a program needn't handle non-finite values.
Results may differ from the reference program's by a relative error of at most 0.0003.
Values sent between devices are 32-bit elements; how exact they have to be, the bound alone decides.
No kernel may reach another device: no remote copies, remote signals or barrier semaphores. Data moves between devices by JAX's collectives and lax.ppermute only.
A program may use at most 64 MiB of HBM per device.

```python
import math
import jax
import jax.numpy as jnp
from jax import lax

MODES = 128
TIME = 65536
STEPS = 2
QUARTETS = 1024


def draw_field(key, part):
    first_key = jax.random.fold_in(key, 0)
    ramp = lax.iota(jnp.float32, TIME) / TIME
    envelope = 0.6 * (1.0 + 2.0 * ramp)
    values = jnp.clip(0.5 * jax.random.normal(first_key, (2, MODES, TIME), jnp.float32), -1.0, 1.0)
    return (values * envelope).astype(jnp.float32)


def set_ends(array, key, low, top_value):
    shape = array.shape
    index_at = [jax.random.randint(jax.random.fold_in(key, axis), (), 0, shape[axis]) for axis in range(len(shape))]
    array = array.at[tuple(index_at)].set(low)
    longest = shape.index(max(shape))
    index_at[longest] = (index_at[longest] + 1) % shape[longest]
    return array.at[tuple(index_at)].set(top_value)


def block_levels(own_key, extent, cuts, low, largest):
    def one(position, shards_of):
        heights = jax.random.uniform(jax.random.fold_in(jax.random.fold_in(own_key, 6), position), (shards_of,), jnp.float32, low / len(cuts), largest / len(cuts))
        return jnp.repeat(jnp.exp(heights), extent[position] // shards_of).reshape((-1,) + (1,) * (len(extent) - position - 1))

    factor_of = one(*cuts[0])
    for cut in cuts[1:]:
        factor_of = factor_of * one(*cut)
    return factor_of


def bell_draw(rng, dims, scale, reach, dtype=jnp.bfloat16):
    return jnp.clip(scale * jax.random.normal(rng, dims, jnp.float32), -reach, reach).astype(dtype)


def setup_inputs(seed: int = 0) -> dict:
    seeds = jax.random.split(jax.random.key(seed), 5)
    return {
        "field": draw_field(jax.random.fold_in(seeds[4], 71), 0),
        "beta": jnp.clip(jax.random.uniform(seeds[1], (3, MODES), jnp.float32, -1.0, 1.0) * block_levels(seeds[1], (3, MODES), ((1, 32),), -0.4, 0.0), -1.0, 1.0),
        "quartets": set_ends(jax.random.randint(seeds[2], (4, QUARTETS), 0, MODES), jax.random.fold_in(seeds[2], 1), 0, MODES - 1).astype(jnp.int32),
        "intersections": bell_draw(seeds[3], (QUARTETS,), 0.03, 0.12, jnp.float32),
    }


epsilon = 1e-06

def phase_of(offset, slope, curve, frequency):
    return math.pi * offset + 300.0 * slope * frequency + 3000.0 * curve * frequency * frequency

def triple_product(left_field, middle_field, conj_field):
    prod_re = left_field[0] * middle_field[0] - left_field[1] * middle_field[1]
    prod_im = left_field[0] * middle_field[1] + left_field[1] * middle_field[0]
    out_re = prod_re * conj_field[0] + prod_im * conj_field[1]
    out_im = prod_im * conj_field[0] - prod_re * conj_field[1]
    return (out_re, out_im)

def kerr_term(fields, quartets, intersections):
    blocks = quartets.shape[1] // 128
    grouped = quartets.reshape(4, blocks, 128).transpose(1, 0, 2)
    weights = intersections.reshape(blocks, 128)

    def accumulate(running, block_item):
        indices, weight = block_item
        out_re, out_im = triple_product(fields[:, indices[1], :], fields[:, indices[2], :], fields[:, indices[3], :])
        contrib = jnp.stack([weight[:, None] * -out_im, weight[:, None] * out_re])
        return (running.at[:, indices[0], :].add(contrib), None)
    running, unused = lax.scan(accumulate, jnp.zeros_like(fields), (grouped, weights))
    return running

def reference(field, beta, quartets, intersections):
    sample_index = lax.iota(jnp.int32, TIME)
    signed = jnp.where(sample_index < TIME // 2, sample_index, sample_index - TIME)
    frequency = signed.astype(jnp.float32) / (TIME / 2)
    angle = phase_of(beta[0][:, None], beta[1][:, None], beta[2][:, None], frequency[None, :])
    rotor = lax.complex(jnp.cos(angle), jnp.sin(angle))
    error_rows = []
    for step_index in range(STEPS):
        spectrum = jnp.fft.fft(lax.complex(field[0], field[1]), axis=-1) * rotor
        moved = jnp.fft.ifft(spectrum, axis=-1)
        linear = jnp.stack([jnp.real(moved), jnp.imag(moved)])
        first = kerr_term(linear, quartets, intersections)
        second = kerr_term(linear + first, quartets, intersections)
        field = linear + 0.5 * (first + second)
        estimate = 0.5 * (second - first)
        error_sq = lax.optimization_barrier(jnp.sum(estimate * estimate, axis=(0, 2)))
        field_sq = lax.optimization_barrier(jnp.sum(field * field, axis=(0, 2)))
        error_rows.append(jnp.sqrt(error_sq / (field_sq + epsilon)))
    return (field, jnp.stack(error_rows))
```

```python
import functools
import math

import jax
import jax.numpy as jnp
import ml_dtypes
import numpy as np
from jax import lax
from jax.experimental import pallas as pl
from jax.experimental.pallas import tpu as pltpu
from jax.sharding import Mesh
from jax.sharding import PartitionSpec as P

STEPS = 2
LANES = 128
TIME = 65536
QUARTER = TIME // 4
TILE = 256
EPSILON = 1e-06
F32 = jnp.float32
BF16 = jnp.bfloat16


def two_parts(table):
    high = table.astype(ml_dtypes.bfloat16)
    low = (table - high.astype(np.float64)).astype(ml_dtypes.bfloat16)
    return (high, low)


def rows_table(table):
    high, low = two_parts(table)
    return np.concatenate([high, high, low], axis=1)


def lanes_table(table):
    high, low = two_parts(table)
    return np.concatenate([high, high, low], axis=0)


@functools.cache
def host_tables():
    index = np.arange(LANES)
    wave = np.exp(-2j * math.pi / LANES * (index[:, None] * index[None, :] % LANES))
    ahead = np.block([[wave.real, -wave.imag], [wave.imag, wave.real]])
    back = np.block([[wave.real, wave.imag], [-wave.imag, wave.real]])

    def row_order(place):
        return np.array([ri * LANES + p for p, ri in place])

    first_order = row_order(
        [
            (v2 * 32 + zb * 8 + rest, ri)
            for zb in range(4)
            for v2 in range(4)
            for ri in range(2)
            for rest in range(8)
        ]
    )
    later_order = row_order(
        [(v * 16 + w, ri) for w in range(16) for ri in range(2) for v in range(8)]
    )
    small = np.exp(-2j * math.pi / QUARTER * (index[:, None] * index[None, :] % QUARTER))

    def twist(place):
        angles = np.arange(4)[1:, None, None] * place[None]
        turned = np.exp(-2j * math.pi / TIME * (angles % TIME))
        return np.stack([turned.real, turned.imag], axis=1)

    rest = np.arange(8)[:, None] * LANES + index[None, :]
    entry = np.stack(
        [
            np.stack([twist(v2 * 4096 + zb * 1024 + rest) for v2 in range(4)])
            for zb in range(4)
        ]
    )
    v = np.arange(8)[:, None] * 2048 + index[None, :]
    middle = np.stack([twist(v + w * LANES) for w in range(16)])
    return {
        "first": rows_table(ahead[:, first_order]),
        "later": rows_table(ahead[:, later_order]),
        "ahead": lanes_table(ahead.T),
        "back": lanes_table(back.T),
        "leave": rows_table(back[later_order] / TIME),
        "small": np.stack([small.real, small.imag]).astype(np.float32),
        "entry": entry.astype(np.float32),
        "middle": middle.astype(np.float32),
    }


def split(array):
    high = array.astype(BF16)
    return (high, (array - high.astype(F32)).astype(BF16))


def dot(left, right):
    return jnp.dot(left, right, preferred_element_type=F32)


def from_left(table, array):
    high, low = split(array)
    return dot(table, jnp.concatenate([high, low, high], axis=0))


def from_right(array, table):
    high, low = split(array)
    return dot(jnp.concatenate([high, low, high], axis=1), table)


def enter_kernel(field_ref, out_ref):
    for ri in range(2):
        for tile in range(32):
            zb, rest = divmod(tile, 8)
            out_ref[pl.ds(zb * 16 + ri * 8 + rest, 4, stride=64), :] = field_ref[
                ri, :, tile * LANES : (tile + 1) * LANES
            ]


def radix_ahead(x):
    (r0, i0), (r1, i1), (r2, i2), (r3, i3) = x
    sr, si, dr, di = r0 + r2, i0 + i2, r0 - r2, i0 - i2
    tr, ti, ur, ui = r1 + r3, i1 + i3, r1 - r3, i1 - i3
    return [(sr + tr, si + ti), (dr + ui, di - ur), (sr - tr, si - ti), (dr - ui, di + ur)]


def radix_back(x):
    out = radix_ahead(x)
    return [out[0], out[3], out[2], out[1]]


def first_radix_kernel(zb_ref, x_ref, twist_ref, out_ref):
    for v2 in range(4):
        at = [a * 64 + v2 * 16 for a in range(4)]
        y = radix_ahead([(x_ref[b : b + 8, :], x_ref[b + 8 : b + 16, :]) for b in at])
        for f in range(4):
            re, im = y[f]
            if f:
                c, s = twist_ref[0, v2, f - 1, 0], twist_ref[0, v2, f - 1, 1]
                re, im = (re * c - im * s, re * s + im * c)
            out_ref[at[f] : at[f] + 8, :] = re
            out_ref[at[f] + 8 : at[f] + 16, :] = im


def ahead_kernel(w_ref, x_ref, twist_ref, out_ref):
    for low in range(4):
        y = radix_ahead(
            [
                tuple(x_ref[pl.ds(a * 64 + low * 2 + ri, 8, stride=8), :] for ri in range(2))
                for a in range(4)
            ]
        )
        for f in range(4):
            re, im = y[f]
            if f:
                c, s = twist_ref[0, f - 1, 0], twist_ref[0, f - 1, 1]
                re, im = (re * c - im * s, re * s + im * c)
            at = low * 64 + f * 16
            out_ref[at : at + 8, :] = re
            out_ref[at + 8 : at + 16, :] = im


def back_kernel(w_ref, x_ref, twist_ref, out_ref):
    for low in range(4):
        y = []
        for f in range(4):
            at = low * 64 + f * 16
            re, im = (x_ref[at : at + 8, :], x_ref[at + 8 : at + 16, :])
            if f:
                c, s = twist_ref[0, f - 1, 0], twist_ref[0, f - 1, 1]
                re, im = (re * c + im * s, im * c - re * s)
            y.append((re, im))
        for a, pair in enumerate(radix_back(y)):
            for ri in range(2):
                out_ref[pl.ds(a * 64 + low * 2 + ri, 8, stride=8), :] = pair[ri]


def cosine_and_sine(angle):
    scaled = angle * (2.0 / math.pi)
    turns = (scaled + jnp.where(scaled >= 0.0, 0.5, -0.5)).astype(jnp.int32)
    count = turns.astype(F32)
    x = angle - count * 1.5703125
    x = x - count * 4.837512969970703125e-4
    x = x - count * 7.5497899548918822e-8
    z = x * x
    sine = ((-1.9515295891e-4 * z + 8.3321608736e-3) * z - 1.6666654611e-1) * z * x + x
    cosine = (
        (2.443315711809948e-5 * z - 1.388731625493765e-3) * z + 4.166664568298827e-2
    ) * z * z - 0.5 * z + 1.0
    quarter = turns & 3
    odd = (quarter & 1) == 1
    c = jnp.where(odd, sine, cosine)
    s = jnp.where(odd, cosine, sine)
    c = jnp.where((quarter == 1) | (quarter == 2), -c, c)
    s = jnp.where(quarter >= 2, -s, s)
    return (c, s)


def spectral_kernel(
    place_ref, beta_ref, x_ref, into_ref, ahead_ref, back_ref, leave_ref, small_ref, out_ref
):
    low, f = (place_ref[0], place_ref[1])
    offset, slope, curve = (beta_ref[k, low] for k in range(3))
    shape = (LANES, LANES)
    wave = 4 * (
        lax.broadcasted_iota(jnp.int32, shape, 0)
        + LANES * lax.broadcasted_iota(jnp.int32, shape, 1)
    )
    wave = wave + f
    signed = jnp.where(wave < TIME // 2, wave, wave - TIME)
    frequency = signed.astype(F32) * (1.0 / (TIME / 2))
    angle = (
        math.pi * offset
        + 300.0 * slope * frequency
        + 3000.0 * curve * frequency * frequency
    )
    cosine, sine = cosine_and_sine(angle)
    small_re, small_im = (small_ref[0], small_ref[1])

    y = from_left(into_ref[...], x_ref[...])
    re, im = (y[:LANES], y[LANES:])
    re, im = (re * small_re - im * small_im, re * small_im + im * small_re)
    y = from_right(jnp.concatenate([re, im], axis=1), ahead_ref[...])
    re, im = (y[:, :LANES], y[:, LANES:])
    re, im = (re * cosine - im * sine, re * sine + im * cosine)
    y = from_right(jnp.concatenate([re, im], axis=1), back_ref[...])
    re, im = (y[:, :LANES], y[:, LANES:])
    re, im = (re * small_re + im * small_im, im * small_re - re * small_im)
    out_ref[...] = from_left(leave_ref[...], jnp.concatenate([re, im], axis=0))


def one_hot(row, count):
    ids = lax.broadcasted_iota(jnp.int32, (count, row.shape[1]), 0)
    return jnp.where(row == ids, 1.0, 0.0).astype(BF16)


def kerr_term(fields, quartets_ref, weights_ref):
    size = fields.shape[0] // 2
    parts = jnp.concatenate(split(fields), axis=1)
    total = None
    for start in range(0, quartets_ref.shape[1], TILE):
        here = slice(start, start + TILE)
        hot = [one_hot(quartets_ref[k : k + 1, here], fields.shape[1]) for k in range(4)]
        (lr, li), (mr, mi), (nr, ni) = (
            (y[:size], y[size:])
            for y in (dot(parts, jnp.concatenate([hot[k]] * 2, axis=0)) for k in (1, 2, 3))
        )
        weight = weights_ref[:, here]
        pr, pi = (lr * mr - li * mi, lr * mi + li * mr)
        pr, pi = (pr * weight, pi * weight)
        out_re, out_im = (pr * nr + pi * ni, pi * nr - pr * ni)
        terms = jnp.concatenate(split(jnp.concatenate([-out_im, out_re], axis=0)), axis=1)
        added = lax.dot_general(
            terms,
            jnp.concatenate([hot[0]] * 2, axis=1),
            (((1,), (1,)), ((), ())),
            preferred_element_type=F32,
        )
        total = added if total is None else total + added
    return total


def kerr_kernel(last, x_ref, quartets_ref, weights_ref, *refs):
    modes = x_ref.shape[0] // 2
    linear = jnp.concatenate(
        [x_ref[pl.ds(ri, modes, stride=2), :].T for ri in range(2)], axis=0
    )
    first = kerr_term(linear, quartets_ref, weights_ref)
    second = kerr_term(linear + first, quartets_ref, weights_ref)
    updated = linear + 0.5 * (first + second)
    estimate = 0.5 * (second - first)
    sums = [jnp.sum(y * y, axis=0, keepdims=True) for y in (estimate, updated)]
    if not last:
        out_ref, sums_ref = refs
        for ri in range(2):
            out_ref[pl.ds(ri, modes, stride=2), :] = updated[ri * LANES : (ri + 1) * LANES].T
        sums_ref[0:1, :] = sums[0]
        sums_ref[1:2, :] = sums[1]
        return
    before_ref, out_ref, held_ref = refs
    for ri in range(2):
        held_ref[pl.ds(ri, modes, stride=2), :] = updated[ri * LANES : (ri + 1) * LANES].T
    norms = jnp.concatenate([before_ref[0:2, :], *sums], axis=0)
    for group in range(modes // 4):
        out_ref[group * 12 : group * 12 + 8, :] = held_ref[group * 8 : group * 8 + 8, :]
        out_ref[group * 12 + 8 : group * 12 + 12, :] = norms


def regroup_kernel(group_ref, x_ref, out_ref):
    norms = x_ref[8:12, :]
    for source in range(1, 32):
        norms = norms + x_ref[source * 12 + 8 : source * 12 + 12, :]
    norms = pltpu.roll(norms, (LANES - 4 * group_ref[0]) % LANES, 1)
    lane = lax.broadcasted_iota(jnp.int32, (1, LANES), 1)
    own = jnp.where(lane < 4, norms[0:1, :], 0.0)
    for k in range(1, 4):
        moved = pltpu.roll(norms[k : k + 1, :], 4 * k, 1)
        own = jnp.where((lane >= 4 * k) & (lane < 4 * k + 4), moved, own)
    for target in range(16):
        for half in range(2):
            source = target * 2 + half
            at = target * 17 + half * 8
            out_ref[at : at + 8, :] = x_ref[source * 12 : source * 12 + 8, :]
        out_ref[target * 17 + 16 : target * 17 + 17, :] = own


def leave_kernel(x_ref, field_ref, errors_ref):
    norms = x_ref[16:17, :]
    for source in range(1, 16):
        norms = norms + x_ref[source * 17 + 16 : source * 17 + 17, :]
    size = pltpu.roll(norms, LANES - 4, 1)
    ratio = jnp.sqrt(norms / (size + EPSILON))
    errors_ref[0:1, :] = ratio[:, 0:4]
    errors_ref[1:2, :] = ratio[:, 8:12]
    for source in range(16):
        for half in range(2):
            tile = half * 16 + source
            for ri in range(2):
                field_ref[ri, :, tile * LANES : (tile + 1) * LANES] = x_ref[
                    pl.ds(source * 17 + half * 8 + ri, 4, stride=2), :
                ]


def rows_of(count):
    return jax.ShapeDtypeStruct((count, LANES), F32)


def picked(kernel, index, array, table, tail):
    zeros = (0,) * len(tail)
    return pl.pallas_call(
        kernel,
        out_shape=rows_of(array.shape[0]),
        grid_spec=pltpu.PrefetchScalarGridSpec(
            num_scalar_prefetch=1,
            grid=(1,),
            in_specs=[
                pl.BlockSpec(array.shape, lambda i, at: (0, 0)),
                pl.BlockSpec((1, *tail), lambda i, at: (at[0], *zeros)),
            ],
            out_specs=pl.BlockSpec(array.shape, lambda i, at: (0, 0)),
        ),
    )(index, array, table)


def exchange(array, axes, peers):
    tiles = array.reshape(peers, array.shape[0] // peers, LANES)
    return lax.all_to_all(tiles, axes, 0, 0, tiled=True).reshape(array.shape)


def shards(field, beta, quartets, intersections):
    tables = {name: jnp.asarray(value) for name, value in host_tables().items()}
    group = lax.axis_index("mode").astype(jnp.int32)[None]
    th, tl = (lax.axis_index("th"), lax.axis_index("tl"))
    place = jnp.stack([th, tl]).astype(jnp.int32)
    low_place = tl.astype(jnp.int32)[None]
    whole_place = (th * 4 + tl).astype(jnp.int32)[None]
    weights = intersections.reshape(1, -1)
    along, across = (("th", "tl"), "mode")
    vmem = pl.BlockSpec(memory_space=pltpu.VMEM)
    smem = pl.BlockSpec(memory_space=pltpu.SMEM)
    limit = pltpu.CompilerParams(vmem_limit_bytes=48 * 1024 * 1024)

    def spectral(state, into):
        return pl.pallas_call(
            spectral_kernel,
            out_shape=rows_of(256),
            in_specs=[smem, smem] + [vmem] * 6,
            out_specs=vmem,
            compiler_params=limit,
        )(place, beta, state, into, tables["ahead"], tables["back"], tables["leave"], tables["small"])

    state = pl.pallas_call(
        enter_kernel, out_shape=rows_of(256), in_specs=[vmem], out_specs=vmem
    )(field)
    state = exchange(state, along, 16)
    state = picked(first_radix_kernel, low_place, state, tables["entry"], (4, 3, 2, 8, LANES))
    state = exchange(state, "tl", 4)
    norms = []
    for step in range(STEPS):
        last = step == STEPS - 1
        state = spectral(state, tables["later" if step else "first"])
        state = exchange(state, along, 16)
        state = picked(back_kernel, whole_place, state, tables["middle"], (3, 2, 8, LANES))
        state = exchange(state, across, 32)
        out = pl.pallas_call(
            functools.partial(kerr_kernel, last),
            out_shape=rows_of(384) if last else (rows_of(256), rows_of(8)),
            in_specs=[vmem] * (3 + len(norms)),
            out_specs=vmem if last else (vmem, vmem),
            scratch_shapes=[pltpu.VMEM((256, LANES), F32)] if last else [],
            compiler_params=limit,
        )(state, quartets, weights, *norms)
        if last:
            state = exchange(out, across, 32)
            break
        state, norm = out
        norms.append(norm)
        state = exchange(state, across, 32)
        state = picked(ahead_kernel, whole_place, state, tables["middle"], (3, 2, 8, LANES))
        state = exchange(state, along, 16)
    state = pl.pallas_call(
        regroup_kernel, out_shape=rows_of(272), in_specs=[smem, vmem], out_specs=vmem
    )(group, state)
    state = exchange(state, along, 16)
    return pl.pallas_call(
        leave_kernel,
        out_shape=(
            jax.ShapeDtypeStruct(field.shape, F32),
            jax.ShapeDtypeStruct((STEPS, field.shape[1]), F32),
        ),
        in_specs=[vmem],
        out_specs=(vmem, vmem),
    )(state)


def solution(mesh):
    finer = Mesh(mesh.devices.reshape(-1, 4, 4), ("mode", "th", "tl"))
    times = ("th", "tl")
    return jax.shard_map(
        shards,
        mesh=finer,
        in_specs=(P(None, "mode", times), P(None, "mode"), P(), P()),
        out_specs=(P(None, "mode", times), P(None, "mode")),
        check_vma=False,
    )
```

```python
import functools
import math

import jax
import jax.numpy as jnp
import ml_dtypes
import numpy as np
from jax import lax
from jax.experimental import pallas as pl
from jax.experimental.pallas import tpu as pltpu
from jax.sharding import Mesh
from jax.sharding import PartitionSpec as P

STEPS = 2
LANES = 128
TIME = 65536
QUARTER = TIME // 4
TILE = 256
EPSILON = 1e-06
F32 = jnp.float32
BF16 = jnp.bfloat16


def two_parts(table):
    high = table.astype(ml_dtypes.bfloat16)
    low = (table - high.astype(np.float64)).astype(ml_dtypes.bfloat16)
    return np.stack([high, low])


@functools.cache
def host_tables():
    index = np.arange(LANES)
    wave = np.exp(-2j * math.pi / LANES * (index[:, None] * index[None, :] % LANES))
    ahead = np.block([[wave.real, -wave.imag], [wave.imag, wave.real]])
    back = np.block([[wave.real, wave.imag], [-wave.imag, wave.real]])

    def row_order(place):
        return np.array([ri * LANES + p for p, ri in place])

    tile_order = row_order(
        [(v * 16 + w, ri) for w in range(16) for ri in range(2) for v in range(8)]
    )
    small = np.exp(-2j * math.pi / QUARTER * (index[:, None] * index[None, :] % QUARTER))

    def twist(place):
        angles = np.arange(4)[1:, None, None] * place[None]
        turned = np.exp(-2j * math.pi / TIME * (angles % TIME))
        return np.stack([turned.real, turned.imag], axis=1)

    rest = np.array([v0 * 2048 + w * LANES for v0 in range(2) for w in range(4)])
    rest = rest[:, None] + index[None, :]
    entry = np.stack(
        [np.stack([twist(v2 * 4096 + zb * 512 + rest) for v2 in range(4)]) for zb in range(4)]
    )
    v = np.arange(8)[:, None] * 2048 + index[None, :]
    middle = np.stack([twist(v + w * LANES) for w in range(16)])
    return {
        "waves": np.stack(
            [
                two_parts(table)
                for table in (ahead[:, tile_order], ahead.T, back.T, back[tile_order] / TIME)
            ]
        ),
        "small": np.stack([small.real, small.imag]).astype(np.float32),
        "entry": entry.astype(np.float32),
        "middle": middle.astype(np.float32),
    }


def split(array):
    high = array.astype(BF16)
    return (high, (array - high.astype(F32)).astype(BF16))


def dot(left, right):
    return jnp.dot(left, right, preferred_element_type=F32)


def from_left(waves_ref, which, array):
    high, low = split(array)
    return dot(waves_ref[which, 0], high) + (
        dot(waves_ref[which, 0], low) + dot(waves_ref[which, 1], high)
    )


def from_right(array, waves_ref, which):
    high, low = split(array)
    return dot(high, waves_ref[which, 0]) + (
        dot(low, waves_ref[which, 0]) + dot(high, waves_ref[which, 1])
    )


def enter_kernel(field_ref, out_ref):
    for ri in range(2):
        for tile in range(32):
            zb, rest = (tile // 4 % 4, tile // 16 * 4 + tile % 4)
            out_ref[pl.ds(zb * 16 + ri * 8 + rest, 4, stride=64), :] = field_ref[
                ri, :, tile * LANES : (tile + 1) * LANES
            ]


def radix_ahead(x):
    (r0, i0), (r1, i1), (r2, i2), (r3, i3) = x
    sr, si, dr, di = r0 + r2, i0 + i2, r0 - r2, i0 - i2
    tr, ti, ur, ui = r1 + r3, i1 + i3, r1 - r3, i1 - i3
    return [(sr + tr, si + ti), (dr + ui, di - ur), (sr - tr, si - ti), (dr - ui, di + ur)]


def radix_back(x):
    out = radix_ahead(x)
    return [out[0], out[3], out[2], out[1]]


def first_radix_kernel(x_ref, twist_ref, out_ref):
    for v2 in range(4):
        at = [a * 64 + v2 * 16 for a in range(4)]
        y = radix_ahead([(x_ref[b : b + 8, :], x_ref[b + 8 : b + 16, :]) for b in at])
        for f in range(4):
            re, im = y[f]
            if f:
                c, s = twist_ref[v2, f - 1, 0], twist_ref[v2, f - 1, 1]
                re, im = (re * c - im * s, re * s + im * c)
            for ri, part in enumerate((re, im)):
                for v0 in range(2):
                    first = f * 64 + ri * 8 + v2 * 2 + v0
                    out_ref[pl.ds(first, 4, stride=16), :] = part[v0 * 4 : v0 * 4 + 4]


def ahead_kernel(x_ref, twist_ref, out_ref):
    for low in range(4):
        y = radix_ahead(
            [
                tuple(x_ref[pl.ds(a * 64 + low * 2 + ri, 8, stride=8), :] for ri in range(2))
                for a in range(4)
            ]
        )
        for f in range(4):
            re, im = y[f]
            if f:
                c, s = twist_ref[f - 1, 0], twist_ref[f - 1, 1]
                re, im = (re * c - im * s, re * s + im * c)
            at = low * 64 + f * 16
            out_ref[at : at + 8, :] = re
            out_ref[at + 8 : at + 16, :] = im


def back_kernel(x_ref, twist_ref, out_ref):
    for low in range(4):
        y = []
        for f in range(4):
            at = low * 64 + f * 16
            re, im = (x_ref[at : at + 8, :], x_ref[at + 8 : at + 16, :])
            if f:
                c, s = twist_ref[f - 1, 0], twist_ref[f - 1, 1]
                re, im = (re * c + im * s, im * c - re * s)
            y.append((re, im))
        for a, pair in enumerate(radix_back(y)):
            for ri in range(2):
                out_ref[pl.ds(a * 64 + low * 2 + ri, 8, stride=8), :] = pair[ri]


def cosine_and_sine(angle):
    scaled = angle * (2.0 / math.pi)
    turns = (scaled + jnp.where(scaled >= 0.0, 0.5, -0.5)).astype(jnp.int32)
    count = turns.astype(F32)
    x = angle - count * 1.5703125
    x = x - count * 4.837512969970703125e-4
    x = x - count * 7.5497899548918822e-8
    z = x * x
    sine = ((-1.9515295891e-4 * z + 8.3321608736e-3) * z - 1.6666654611e-1) * z * x + x
    cosine = (
        (2.443315711809948e-5 * z - 1.388731625493765e-3) * z + 4.166664568298827e-2
    ) * z * z - 0.5 * z + 1.0
    quarter = turns & 3
    odd = (quarter & 1) == 1
    c = jnp.where(odd, sine, cosine)
    s = jnp.where(odd, cosine, sine)
    c = jnp.where((quarter == 1) | (quarter == 2), -c, c)
    s = jnp.where(quarter >= 2, -s, s)
    return (c, s)


def spectral_kernel(
    place_ref, beta_ref, x_ref, waves_ref, small_ref, out_ref
):
    low, f = (place_ref[0], place_ref[1])
    offset, slope, curve = (beta_ref[k, low] for k in range(3))
    shape = (LANES, LANES)
    wave = 4 * (
        lax.broadcasted_iota(jnp.int32, shape, 0)
        + LANES * lax.broadcasted_iota(jnp.int32, shape, 1)
    )
    wave = wave + f
    signed = jnp.where(wave < TIME // 2, wave, wave - TIME)
    frequency = signed.astype(F32) * (1.0 / (TIME / 2))
    angle = (
        math.pi * offset
        + 300.0 * slope * frequency
        + 3000.0 * curve * frequency * frequency
    )
    cosine, sine = cosine_and_sine(angle)
    small_re, small_im = (small_ref[0], small_ref[1])

    y = from_left(waves_ref, 0, x_ref[...])
    re, im = (y[:LANES], y[LANES:])
    re, im = (re * small_re - im * small_im, re * small_im + im * small_re)
    y = from_right(jnp.concatenate([re, im], axis=1), waves_ref, 1)
    re, im = (y[:, :LANES], y[:, LANES:])
    re, im = (re * cosine - im * sine, re * sine + im * cosine)
    y = from_right(jnp.concatenate([re, im], axis=1), waves_ref, 2)
    re, im = (y[:, :LANES], y[:, LANES:])
    re, im = (re * small_re + im * small_im, im * small_re - re * small_im)
    out_ref[...] = from_left(waves_ref, 3, jnp.concatenate([re, im], axis=0))


def one_hot(row, count):
    ids = lax.broadcasted_iota(jnp.int32, (count, row.shape[1]), 0)
    return jnp.where(row == ids, 1.0, 0.0).astype(BF16)


def kerr_term(fields, quartets_ref, weights_ref):
    size = fields.shape[0] // 2
    parts = jnp.concatenate(split(fields), axis=1)
    total = None
    for start in range(0, quartets_ref.shape[1], TILE):
        here = slice(start, start + TILE)
        hot = [one_hot(quartets_ref[k : k + 1, here], fields.shape[1]) for k in range(4)]
        (lr, li), (mr, mi), (nr, ni) = (
            (y[:size], y[size:])
            for y in (dot(parts, jnp.concatenate([hot[k]] * 2, axis=0)) for k in (1, 2, 3))
        )
        weight = weights_ref[:, here]
        pr, pi = (lr * mr - li * mi, lr * mi + li * mr)
        pr, pi = (pr * weight, pi * weight)
        out_re, out_im = (pr * nr + pi * ni, pi * nr - pr * ni)
        terms = jnp.concatenate(split(jnp.concatenate([-out_im, out_re], axis=0)), axis=1)
        added = lax.dot_general(
            terms,
            jnp.concatenate([hot[0]] * 2, axis=1),
            (((1,), (1,)), ((), ())),
            preferred_element_type=F32,
        )
        total = added if total is None else total + added
    return total


def kerr_kernel(last, x_ref, quartets_ref, weights_ref, *refs):
    modes = x_ref.shape[0] // 2
    linear = jnp.concatenate(
        [x_ref[pl.ds(ri, modes, stride=2), :].T for ri in range(2)], axis=0
    )
    first = kerr_term(linear, quartets_ref, weights_ref)
    second = kerr_term(linear + first, quartets_ref, weights_ref)
    updated = linear + 0.5 * (first + second)
    estimate = 0.5 * (second - first)
    sums = [jnp.sum(y * y, axis=0, keepdims=True) for y in (estimate, updated)]
    if not last:
        out_ref, sums_ref = refs
        for ri in range(2):
            out_ref[pl.ds(ri, modes, stride=2), :] = updated[ri * LANES : (ri + 1) * LANES].T
        sums_ref[0:1, :] = sums[0]
        sums_ref[1:2, :] = sums[1]
        return
    before_ref, out_ref, held_ref = refs
    for ri in range(2):
        held_ref[pl.ds(ri, modes, stride=2), :] = updated[ri * LANES : (ri + 1) * LANES].T
    norms = jnp.concatenate([before_ref[0:2, :], *sums], axis=0)
    for group in range(modes // 4):
        out_ref[group * 12 : group * 12 + 8, :] = held_ref[group * 8 : group * 8 + 8, :]
        out_ref[group * 12 + 8 : group * 12 + 12, :] = norms


def regroup_kernel(group_ref, x_ref, out_ref):
    norms = x_ref[8:12, :]
    for source in range(1, 32):
        norms = norms + x_ref[source * 12 + 8 : source * 12 + 12, :]
    norms = pltpu.roll(norms, (LANES - 4 * group_ref[0]) % LANES, 1)
    lane = lax.broadcasted_iota(jnp.int32, (1, LANES), 1)
    own = jnp.where(lane < 4, norms[0:1, :], 0.0)
    for k in range(1, 4):
        moved = pltpu.roll(norms[k : k + 1, :], 4 * k, 1)
        own = jnp.where((lane >= 4 * k) & (lane < 4 * k + 4), moved, own)
    for target in range(16):
        for half in range(2):
            source = target * 2 + half
            at = target * 17 + half * 8
            out_ref[at : at + 8, :] = x_ref[source * 12 : source * 12 + 8, :]
        out_ref[target * 17 + 16 : target * 17 + 17, :] = own


def leave_kernel(x_ref, field_ref, errors_ref):
    norms = x_ref[16:17, :]
    for source in range(1, 16):
        norms = norms + x_ref[source * 17 + 16 : source * 17 + 17, :]
    size = pltpu.roll(norms, LANES - 4, 1)
    ratio = jnp.sqrt(norms / (size + EPSILON))
    errors_ref[0:1, :] = ratio[:, 0:4]
    errors_ref[1:2, :] = ratio[:, 8:12]
    for source in range(16):
        for half in range(2):
            tile = half * 16 + source
            for ri in range(2):
                field_ref[ri, :, tile * LANES : (tile + 1) * LANES] = x_ref[
                    pl.ds(source * 17 + half * 8 + ri, 4, stride=2), :
                ]


def rows_of(count):
    return jax.ShapeDtypeStruct((count, LANES), F32)


def exchange(array, axes, peers):
    rows = array.shape[0] // peers
    tile = 8 if rows % 8 == 0 else 1
    tiles = array.reshape(peers, rows // tile, tile, LANES)
    return lax.all_to_all(tiles, axes, 0, 0, tiled=True).reshape(array.shape)


def shards(field, beta, quartets, intersections):
    tables = {name: jnp.asarray(value) for name, value in host_tables().items()}
    group = lax.axis_index("mode").astype(jnp.int32)[None]
    th, tl = (lax.axis_index("th"), lax.axis_index("tl"))
    place = jnp.stack([th, tl]).astype(jnp.int32)
    entry = lax.dynamic_index_in_dim(tables["entry"], tl, keepdims=False)
    middle = lax.dynamic_index_in_dim(tables["middle"], th * 4 + tl, keepdims=False)
    weights = intersections.reshape(1, -1)
    along, across = (("th", "tl"), "mode")
    vmem = pl.BlockSpec(memory_space=pltpu.VMEM)
    smem = pl.BlockSpec(memory_space=pltpu.SMEM)
    limit = pltpu.CompilerParams(vmem_limit_bytes=16 * 1024 * 1024)

    def picked(kernel, state, table):
        return pl.pallas_call(
            kernel,
            out_shape=rows_of(256),
            in_specs=[vmem, vmem],
            out_specs=vmem,
            compiler_params=limit,
        )(state, table)

    def spectral(state):
        return pl.pallas_call(
            spectral_kernel,
            out_shape=rows_of(256),
            in_specs=[smem, smem] + [vmem] * 3,
            out_specs=vmem,
            compiler_params=limit,
        )(place, beta, state, tables["waves"], tables["small"])

    state = pl.pallas_call(
        enter_kernel,
        out_shape=rows_of(256),
        in_specs=[vmem],
        out_specs=vmem,
        compiler_params=limit,
    )(field)
    state = exchange(state, along, 16)
    state = picked(first_radix_kernel, state, entry)
    state = exchange(state, "tl", 4)
    norms = []
    for step in range(STEPS):
        last = step == STEPS - 1
        state = spectral(state)
        state = exchange(state, along, 16)
        state = picked(back_kernel, state, middle)
        state = exchange(state, across, 32)
        out = pl.pallas_call(
            functools.partial(kerr_kernel, last),
            out_shape=rows_of(384) if last else (rows_of(256), rows_of(8)),
            in_specs=[vmem] * (3 + len(norms)),
            out_specs=vmem if last else (vmem, vmem),
            scratch_shapes=[pltpu.VMEM((256, LANES), F32)] if last else [],
            compiler_params=limit,
        )(state, quartets, weights, *norms)
        if last:
            state = exchange(out, across, 32)
            break
        state, norm = out
        norms.append(norm)
        state = exchange(state, across, 32)
        state = picked(ahead_kernel, state, middle)
        state = exchange(state, along, 16)
    state = pl.pallas_call(
        regroup_kernel,
        out_shape=rows_of(272),
        in_specs=[smem, vmem],
        out_specs=vmem,
        compiler_params=limit,
    )(group, state)
    state = exchange(state, along, 16)
    return pl.pallas_call(
        leave_kernel,
        out_shape=(
            jax.ShapeDtypeStruct(field.shape, F32),
            jax.ShapeDtypeStruct((STEPS, field.shape[1]), F32),
        ),
        in_specs=[vmem],
        out_specs=(vmem, vmem),
        compiler_params=limit,
    )(state)


def solution(mesh):
    finer = Mesh(mesh.devices.reshape(-1, 4, 4), ("mode", "th", "tl"))
    times = ("th", "tl")
    return jax.shard_map(
        shards,
        mesh=finer,
        in_specs=(P(None, "mode", times), P(None, "mode"), P(), P()),
        out_specs=(P(None, "mode", times), P(None, "mode")),
        check_vma=False,
    )
```

```python
import functools
import math

import jax
import jax.numpy as jnp
import ml_dtypes
import numpy as np
from jax import lax
from jax.experimental import pallas as pl
from jax.experimental.pallas import tpu as pltpu
from jax.sharding import Mesh
from jax.sharding import PartitionSpec as P

STEPS = 2
LANES = 128
TIME = 65536
QUARTER = TIME // 4
TILE = 256
EPSILON = 1e-06
F32 = jnp.float32
BF16 = jnp.bfloat16


def two_parts(table):
    high = table.astype(ml_dtypes.bfloat16)
    low = (table - high.astype(np.float64)).astype(ml_dtypes.bfloat16)
    return np.stack([high, low])


@functools.cache
def host_waves():
    index = np.arange(LANES)
    wave = np.exp(-2j * math.pi / LANES * (index[:, None] * index[None, :] % LANES))
    ahead = np.block([[wave.real, -wave.imag], [wave.imag, wave.real]])
    back = np.block([[wave.real, wave.imag], [-wave.imag, wave.real]])

    def row_order(place):
        return np.array([ri * LANES + p for p, ri in place])

    tile_order = row_order(
        [(v * 16 + w, ri) for w in range(16) for ri in range(2) for v in range(8)]
    )
    tables = (ahead[:, tile_order], ahead.T, back.T, back[tile_order] / TIME)
    return np.stack([two_parts(table) for table in tables])


def split(array):
    high = array.astype(BF16)
    return (high, (array - high.astype(F32)).astype(BF16))


def dot(left, right):
    return jnp.dot(left, right, preferred_element_type=F32)


def from_left(waves_ref, which, array):
    high, low = split(array)
    return dot(waves_ref[which, 0], high) + (
        dot(waves_ref[which, 0], low) + dot(waves_ref[which, 1], high)
    )


def from_right(array, waves_ref, which):
    high, low = split(array)
    return dot(high, waves_ref[which, 0]) + (
        dot(low, waves_ref[which, 0]) + dot(high, waves_ref[which, 1])
    )


def small_cosine_and_sine(x):
    z = x * x
    sine = ((-1.9515295891e-4 * z + 8.3321608736e-3) * z - 1.6666654611e-1) * z * x + x
    cosine = (
        (2.443315711809948e-5 * z - 1.388731625493765e-3) * z + 4.166664568298827e-2
    ) * z * z - 0.5 * z + 1.0
    return (cosine, sine)


def in_quarter(turns, cosine, sine):
    quarter = turns & 3
    odd = (quarter & 1) == 1
    c = jnp.where(odd, sine, cosine)
    s = jnp.where(odd, cosine, sine)
    c = jnp.where((quarter == 1) | (quarter == 2), -c, c)
    s = jnp.where(quarter >= 2, -s, s)
    return (c, s)


def cosine_and_sine(angle):
    scaled = angle * (2.0 / math.pi)
    turns = (scaled + jnp.where(scaled >= 0.0, 0.5, -0.5)).astype(jnp.int32)
    count = turns.astype(F32)
    x = angle - count * 1.5703125
    x = x - count * 4.837512969970703125e-4
    x = x - count * 7.5497899548918822e-8
    return in_quarter(turns, *small_cosine_and_sine(x))


def twist(number):
    turns = (number + TIME // 8) // QUARTER
    rest = (number - turns * QUARTER).astype(F32)
    return in_quarter(turns, *small_cosine_and_sine(rest * (2.0 * math.pi / TIME)))


def row_and_lane():
    return (lax.broadcasted_iota(jnp.int32, (8, LANES), axis) for axis in range(2))


def enter_kernel(field_ref, out_ref):
    for ri in range(2):
        for tile in range(32):
            zb, rest = (tile // 4 % 4, tile // 16 * 4 + tile % 4)
            out_ref[pl.ds(zb * 16 + ri * 8 + rest, 4, stride=64), :] = field_ref[
                ri, :, tile * LANES : (tile + 1) * LANES
            ]


def radix_ahead(x):
    (r0, i0), (r1, i1), (r2, i2), (r3, i3) = x
    sr, si, dr, di = r0 + r2, i0 + i2, r0 - r2, i0 - i2
    tr, ti, ur, ui = r1 + r3, i1 + i3, r1 - r3, i1 - i3
    return [(sr + tr, si + ti), (dr + ui, di - ur), (sr - tr, si - ti), (dr - ui, di + ur)]


def radix_back(x):
    out = radix_ahead(x)
    return [out[0], out[3], out[2], out[1]]


def turned_back(pair, c, s):
    re, im = pair
    return (re * c + im * s, im * c - re * s)


def turned(pair, c, s):
    return turned_back(pair, c, -s)


def first_radix_kernel(zb_ref, x_ref, out_ref):
    row, lane = row_and_lane()
    place = (row // 4) * 2048 + (row % 4) * LANES + lane + zb_ref[0] * 512
    for v2 in range(4):
        at = [a * 64 + v2 * 16 for a in range(4)]
        y = radix_ahead([(x_ref[b : b + 8, :], x_ref[b + 8 : b + 16, :]) for b in at])
        for f in range(4):
            pair = turned_back(y[f], *twist(f * (place + v2 * 4096))) if f else y[f]
            for ri in range(2):
                for v0 in range(2):
                    first = f * 64 + ri * 8 + v2 * 2 + v0
                    out_ref[pl.ds(first, 4, stride=16), :] = pair[ri][v0 * 4 : v0 * 4 + 4]


def middle_twists(th_ref, tl_ref):
    row, lane = row_and_lane()
    place = row * 2048 + lane + (th_ref[0] * 4 + tl_ref[0]) * LANES
    return [None] + [twist(f * place) for f in range(1, 4)]


def ahead_kernel(th_ref, tl_ref, x_ref, out_ref):
    twists = middle_twists(th_ref, tl_ref)
    for low in range(4):
        y = radix_ahead(
            [
                tuple(x_ref[pl.ds(a * 64 + low * 2 + ri, 8, stride=8), :] for ri in range(2))
                for a in range(4)
            ]
        )
        for f in range(4):
            re, im = turned_back(y[f], *twists[f]) if f else y[f]
            at = low * 64 + f * 16
            out_ref[at : at + 8, :] = re
            out_ref[at + 8 : at + 16, :] = im


def back_kernel(th_ref, tl_ref, x_ref, out_ref):
    twists = middle_twists(th_ref, tl_ref)
    for low in range(4):
        y = []
        for f in range(4):
            at = low * 64 + f * 16
            pair = (x_ref[at : at + 8, :], x_ref[at + 8 : at + 16, :])
            y.append(turned(pair, *twists[f]) if f else pair)
        for a, pair in enumerate(radix_back(y)):
            for ri in range(2):
                out_ref[pl.ds(a * 64 + low * 2 + ri, 8, stride=8), :] = pair[ri]


def spectral_kernel(th_ref, tl_ref, beta_ref, x_ref, waves_ref, out_ref):
    low, f = (th_ref[0], tl_ref[0])
    offset, slope, curve = (beta_ref[k, low] for k in range(3))
    shape = (LANES, LANES)
    row, lane = (lax.broadcasted_iota(jnp.int32, shape, axis) for axis in range(2))
    small = twist(4 * row * lane)
    wave = 4 * (row + LANES * lane) + f
    signed = jnp.where(wave < TIME // 2, wave, wave - TIME)
    frequency = signed.astype(F32) * (1.0 / (TIME / 2))
    angle = (
        math.pi * offset
        + 300.0 * slope * frequency
        + 3000.0 * curve * frequency * frequency
    )
    cosine, sine = cosine_and_sine(angle)

    y = from_left(waves_ref, 0, x_ref[...])
    re, im = turned_back((y[:LANES], y[LANES:]), *small)
    y = from_right(jnp.concatenate([re, im], axis=1), waves_ref, 1)
    re, im = turned((y[:, :LANES], y[:, LANES:]), cosine, sine)
    y = from_right(jnp.concatenate([re, im], axis=1), waves_ref, 2)
    re, im = turned((y[:, :LANES], y[:, LANES:]), *small)
    out_ref[...] = from_left(waves_ref, 3, jnp.concatenate([re, im], axis=0))


def one_hot(row, count):
    ids = lax.broadcasted_iota(jnp.int32, (count, row.shape[1]), 0)
    return jnp.where(row == ids, 1.0, 0.0).astype(BF16)


def kerr_term(fields, quartets_ref, weights_ref):
    size = fields.shape[0] // 2
    parts = jnp.concatenate(split(fields), axis=1)
    total = None
    for start in range(0, quartets_ref.shape[1], TILE):
        here = slice(start, start + TILE)
        hot = [one_hot(quartets_ref[k : k + 1, here], fields.shape[1]) for k in range(4)]
        (lr, li), (mr, mi), (nr, ni) = (
            (y[:size], y[size:])
            for y in (dot(parts, jnp.concatenate([hot[k]] * 2, axis=0)) for k in (1, 2, 3))
        )
        weight = weights_ref[:, here]
        pr, pi = (lr * mr - li * mi, lr * mi + li * mr)
        pr, pi = (pr * weight, pi * weight)
        out_re, out_im = (pr * nr + pi * ni, pi * nr - pr * ni)
        terms = jnp.concatenate(split(jnp.concatenate([-out_im, out_re], axis=0)), axis=1)
        added = lax.dot_general(
            terms,
            jnp.concatenate([hot[0]] * 2, axis=1),
            (((1,), (1,)), ((), ())),
            preferred_element_type=F32,
        )
        total = added if total is None else total + added
    return total


def kerr_kernel(last, x_ref, quartets_ref, weights_ref, *refs):
    modes = x_ref.shape[0] // 2
    linear = jnp.concatenate(
        [x_ref[pl.ds(ri, modes, stride=2), :].T for ri in range(2)], axis=0
    )
    first = kerr_term(linear, quartets_ref, weights_ref)
    second = kerr_term(linear + first, quartets_ref, weights_ref)
    updated = linear + 0.5 * (first + second)
    estimate = 0.5 * (second - first)
    sums = [jnp.sum(y * y, axis=0, keepdims=True) for y in (estimate, updated)]
    if not last:
        out_ref, sums_ref = refs
        for ri in range(2):
            out_ref[pl.ds(ri, modes, stride=2), :] = updated[ri * LANES : (ri + 1) * LANES].T
        sums_ref[0:1, :] = sums[0]
        sums_ref[1:2, :] = sums[1]
        return
    before_ref, out_ref, held_ref = refs
    for ri in range(2):
        held_ref[pl.ds(ri, modes, stride=2), :] = updated[ri * LANES : (ri + 1) * LANES].T
    norms = jnp.concatenate([before_ref[0:2, :], *sums], axis=0)
    for group in range(modes // 4):
        out_ref[group * 12 : group * 12 + 8, :] = held_ref[group * 8 : group * 8 + 8, :]
        out_ref[group * 12 + 8 : group * 12 + 12, :] = norms


def regroup_kernel(group_ref, x_ref, out_ref):
    norms = x_ref[8:12, :]
    for source in range(1, 32):
        norms = norms + x_ref[source * 12 + 8 : source * 12 + 12, :]
    norms = pltpu.roll(norms, (LANES - 4 * group_ref[0]) % LANES, 1)
    lane = lax.broadcasted_iota(jnp.int32, (1, LANES), 1)
    own = jnp.where(lane < 4, norms[0:1, :], 0.0)
    for k in range(1, 4):
        moved = pltpu.roll(norms[k : k + 1, :], 4 * k, 1)
        own = jnp.where((lane >= 4 * k) & (lane < 4 * k + 4), moved, own)
    for target in range(16):
        for half in range(2):
            source = target * 2 + half
            at = target * 17 + half * 8
            out_ref[at : at + 8, :] = x_ref[source * 12 : source * 12 + 8, :]
        out_ref[target * 17 + 16 : target * 17 + 17, :] = own


def leave_kernel(x_ref, field_ref, errors_ref):
    norms = x_ref[16:17, :]
    for source in range(1, 16):
        norms = norms + x_ref[source * 17 + 16 : source * 17 + 17, :]
    size = pltpu.roll(norms, LANES - 4, 1)
    ratio = jnp.sqrt(norms / (size + EPSILON))
    errors_ref[0:1, :] = ratio[:, 0:4]
    errors_ref[1:2, :] = ratio[:, 8:12]
    for source in range(16):
        for half in range(2):
            tile = half * 16 + source
            for ri in range(2):
                field_ref[ri, :, tile * LANES : (tile + 1) * LANES] = x_ref[
                    pl.ds(source * 17 + half * 8 + ri, 4, stride=2), :
                ]


def rows_of(count):
    return jax.ShapeDtypeStruct((count, LANES), F32)


def exchange(array, axes, peers):
    rows = array.shape[0] // peers
    tile = 8 if rows % 8 == 0 else 1
    tiles = array.reshape(peers, rows // tile, tile, LANES)
    return lax.all_to_all(tiles, axes, 0, 0, tiled=True).reshape(array.shape)


def shards(field, beta, quartets, intersections):
    waves = jnp.asarray(host_waves())
    field, group, th, tl = lax.optimization_barrier(
        (field, *(lax.axis_index(a).astype(jnp.int32) for a in ("mode", "th", "tl")))
    )
    group, th, tl = (group[None], th[None], tl[None])
    weights = intersections.reshape(1, -1)
    along, across = (("th", "tl"), "mode")
    vmem = pl.BlockSpec(memory_space=pltpu.VMEM)
    smem = pl.BlockSpec(memory_space=pltpu.SMEM)
    limit = pltpu.CompilerParams(vmem_limit_bytes=16 * 1024 * 1024)

    def placed(kernel, state, *numbers):
        return pl.pallas_call(
            kernel,
            out_shape=rows_of(256),
            in_specs=[smem] * len(numbers) + [vmem],
            out_specs=vmem,
            compiler_params=limit,
        )(*numbers, state)

    def spectral(state):
        return pl.pallas_call(
            spectral_kernel,
            out_shape=rows_of(256),
            in_specs=[smem] * 3 + [vmem] * 2,
            out_specs=vmem,
            compiler_params=limit,
        )(th, tl, beta, state, waves)

    state = pl.pallas_call(
        enter_kernel,
        out_shape=rows_of(256),
        in_specs=[vmem],
        out_specs=vmem,
        compiler_params=limit,
    )(field)
    state = exchange(state, along, 16)
    state = placed(first_radix_kernel, state, tl)
    state = exchange(state, "tl", 4)
    norms = []
    for step in range(STEPS):
        last = step == STEPS - 1
        state = spectral(state)
        state = exchange(state, along, 16)
        state = placed(back_kernel, state, th, tl)
        state = exchange(state, across, 32)
        out = pl.pallas_call(
            functools.partial(kerr_kernel, last),
            out_shape=rows_of(384) if last else (rows_of(256), rows_of(8)),
            in_specs=[vmem] * (3 + len(norms)),
            out_specs=vmem if last else (vmem, vmem),
            scratch_shapes=[pltpu.VMEM((256, LANES), F32)] if last else [],
            compiler_params=limit,
        )(state, quartets, weights, *norms)
        if last:
            state = exchange(out, across, 32)
            break
        state, norm = out
        norms.append(norm)
        state = exchange(state, across, 32)
        state = placed(ahead_kernel, state, th, tl)
        state = exchange(state, along, 16)
    state = pl.pallas_call(
        regroup_kernel,
        out_shape=rows_of(272),
        in_specs=[smem, vmem],
        out_specs=vmem,
        compiler_params=limit,
    )(group, state)
    state = exchange(state, along, 16)
    return pl.pallas_call(
        leave_kernel,
        out_shape=(
            jax.ShapeDtypeStruct(field.shape, F32),
            jax.ShapeDtypeStruct((STEPS, field.shape[1]), F32),
        ),
        in_specs=[vmem],
        out_specs=(vmem, vmem),
        compiler_params=limit,
    )(state)


def solution(mesh):
    finer = Mesh(mesh.devices.reshape(-1, 4, 4), ("mode", "th", "tl"))
    times = ("th", "tl")
    return jax.shard_map(
        shards,
        mesh=finer,
        in_specs=(P(None, "mode", times), P(None, "mode"), P(), P()),
        out_specs=(P(None, "mode", times), P(None, "mode")),
        check_vma=False,
    )
```

```python
import functools
import math

import jax
import jax.numpy as jnp
import ml_dtypes
import numpy as np
from jax import lax
from jax.experimental import pallas as pl
from jax.experimental.pallas import tpu as pltpu
from jax.sharding import Mesh
from jax.sharding import PartitionSpec as P

STEPS = 2
LANES = 128
TIME = 65536
QUARTER = TIME // 4
TILE = 256
EPSILON = 1e-06
F32 = jnp.float32
BF16 = jnp.bfloat16


def two_parts(table):
    high = table.astype(ml_dtypes.bfloat16)
    low = (table - high.astype(np.float64)).astype(ml_dtypes.bfloat16)
    return np.stack([high, low])


@functools.cache
def host_waves():
    index = np.arange(LANES)
    wave = np.exp(-2j * math.pi / LANES * (index[:, None] * index[None, :] % LANES))
    ahead = np.block([[wave.real, -wave.imag], [wave.imag, wave.real]])
    back = np.block([[wave.real, wave.imag], [-wave.imag, wave.real]])

    def row_order(place):
        return np.array([ri * LANES + p for p, ri in place])

    tile_order = row_order(
        [(v * 16 + w, ri) for w in range(16) for ri in range(2) for v in range(8)]
    )
    tables = (ahead[:, tile_order], ahead.T, back.T, back[tile_order] / TIME)
    return np.stack([two_parts(table) for table in tables])


def split(array):
    high = array.astype(BF16)
    return (high, (array - high.astype(F32)).astype(BF16))


def dot(left, right):
    return jnp.dot(left, right, preferred_element_type=F32)


def from_left(waves_ref, which, array):
    high, low = split(array)
    return dot(waves_ref[which, 0], high) + (
        dot(waves_ref[which, 0], low) + dot(waves_ref[which, 1], high)
    )


def from_right(array, waves_ref, which):
    high, low = split(array)
    return dot(high, waves_ref[which, 0]) + (
        dot(low, waves_ref[which, 0]) + dot(high, waves_ref[which, 1])
    )


def small_cosine_and_sine(x):
    z = x * x
    sine = ((-1.9515295891e-4 * z + 8.3321608736e-3) * z - 1.6666654611e-1) * z * x + x
    cosine = (
        (2.443315711809948e-5 * z - 1.388731625493765e-3) * z + 4.166664568298827e-2
    ) * z * z - 0.5 * z + 1.0
    return (cosine, sine)


def in_quarter(turns, cosine, sine):
    quarter = turns & 3
    odd = (quarter & 1) == 1
    c = jnp.where(odd, sine, cosine)
    s = jnp.where(odd, cosine, sine)
    c = jnp.where((quarter == 1) | (quarter == 2), -c, c)
    s = jnp.where(quarter >= 2, -s, s)
    return (c, s)


def cosine_and_sine(angle):
    scaled = angle * (2.0 / math.pi)
    turns = (scaled + jnp.where(scaled >= 0.0, 0.5, -0.5)).astype(jnp.int32)
    count = turns.astype(F32)
    x = angle - count * 1.5703125
    x = x - count * 4.837512969970703125e-4
    x = x - count * 7.5497899548918822e-8
    return in_quarter(turns, *small_cosine_and_sine(x))


def twist(number):
    turns = (number + TIME // 8) // QUARTER
    rest = (number - turns * QUARTER).astype(F32)
    return in_quarter(turns, *small_cosine_and_sine(rest * (2.0 * math.pi / TIME)))


def row_and_lane():
    return (lax.broadcasted_iota(jnp.int32, (8, LANES), axis) for axis in range(2))


def rotor_kernel(th_ref, tl_ref, beta_ref, rotor_ref, small_ref):
    offset, slope, curve = (beta_ref[k, th_ref[0]] for k in range(3))
    shape = (LANES, LANES)
    row, lane = (lax.broadcasted_iota(jnp.int32, shape, axis) for axis in range(2))
    small_ref[0], small_ref[1] = twist(4 * row * lane)
    wave = 4 * (row + LANES * lane) + tl_ref[0]
    signed = jnp.where(wave < TIME // 2, wave, wave - TIME)
    frequency = signed.astype(F32) * (1.0 / (TIME / 2))
    angle = (
        math.pi * offset
        + 300.0 * slope * frequency
        + 3000.0 * curve * frequency * frequency
    )
    rotor_ref[0], rotor_ref[1] = cosine_and_sine(angle)


def enter_kernel(field_ref, after_ref, out_ref):
    for ri in range(2):
        for tile in range(32):
            zb, rest = (tile // 4 % 4, tile // 16 * 4 + tile % 4)
            out_ref[pl.ds(zb * 16 + ri * 8 + rest, 4, stride=64), :] = field_ref[
                ri, :, tile * LANES : (tile + 1) * LANES
            ]


def radix_ahead(x):
    (r0, i0), (r1, i1), (r2, i2), (r3, i3) = x
    sr, si, dr, di = r0 + r2, i0 + i2, r0 - r2, i0 - i2
    tr, ti, ur, ui = r1 + r3, i1 + i3, r1 - r3, i1 - i3
    return [(sr + tr, si + ti), (dr + ui, di - ur), (sr - tr, si - ti), (dr - ui, di + ur)]


def radix_back(x):
    out = radix_ahead(x)
    return [out[0], out[3], out[2], out[1]]


def turned_back(pair, c, s):
    re, im = pair
    return (re * c + im * s, im * c - re * s)


def turned(pair, c, s):
    return turned_back(pair, c, -s)


def first_radix_kernel(zb_ref, x_ref, out_ref):
    row, lane = row_and_lane()
    place = (row // 4) * 2048 + (row % 4) * LANES + lane + zb_ref[0] * 512
    for v2 in range(4):
        at = [a * 64 + v2 * 16 for a in range(4)]
        y = radix_ahead([(x_ref[b : b + 8, :], x_ref[b + 8 : b + 16, :]) for b in at])
        for f in range(4):
            pair = turned_back(y[f], *twist(f * (place + v2 * 4096))) if f else y[f]
            for ri in range(2):
                for v0 in range(2):
                    first = f * 64 + ri * 8 + v2 * 2 + v0
                    out_ref[pl.ds(first, 4, stride=16), :] = pair[ri][v0 * 4 : v0 * 4 + 4]


def middle_twists(th_ref, tl_ref):
    row, lane = row_and_lane()
    place = row * 2048 + lane + (th_ref[0] * 4 + tl_ref[0]) * LANES
    return [None] + [twist(f * place) for f in range(1, 4)]


def ahead_kernel(th_ref, tl_ref, x_ref, out_ref):
    twists = middle_twists(th_ref, tl_ref)
    for low in range(4):
        y = radix_ahead(
            [
                tuple(x_ref[pl.ds(a * 64 + low * 2 + ri, 8, stride=8), :] for ri in range(2))
                for a in range(4)
            ]
        )
        for f in range(4):
            re, im = turned_back(y[f], *twists[f]) if f else y[f]
            at = low * 64 + f * 16
            out_ref[at : at + 8, :] = re
            out_ref[at + 8 : at + 16, :] = im


def back_kernel(th_ref, tl_ref, x_ref, out_ref):
    twists = middle_twists(th_ref, tl_ref)
    for low in range(4):
        y = []
        for f in range(4):
            at = low * 64 + f * 16
            pair = (x_ref[at : at + 8, :], x_ref[at + 8 : at + 16, :])
            y.append(turned(pair, *twists[f]) if f else pair)
        for a, pair in enumerate(radix_back(y)):
            for ri in range(2):
                out_ref[pl.ds(a * 64 + low * 2 + ri, 8, stride=8), :] = pair[ri]


def spectral_kernel(x_ref, rotor_ref, small_ref, waves_ref, out_ref):
    rotor = (rotor_ref[0], rotor_ref[1])
    small = (small_ref[0], small_ref[1])
    y = from_left(waves_ref, 0, x_ref[...])
    re, im = turned_back((y[:LANES], y[LANES:]), *small)
    y = from_right(jnp.concatenate([re, im], axis=1), waves_ref, 1)
    re, im = turned((y[:, :LANES], y[:, LANES:]), *rotor)
    y = from_right(jnp.concatenate([re, im], axis=1), waves_ref, 2)
    re, im = turned((y[:, :LANES], y[:, LANES:]), *small)
    out_ref[...] = from_left(waves_ref, 3, jnp.concatenate([re, im], axis=0))


def one_hots(quartets_ref, modes):
    ids = lax.broadcasted_iota(jnp.int32, (modes, quartets_ref.shape[1]), 0)
    return [
        jnp.where(quartets_ref[k : k + 1, :] == ids, 1.0, 0.0).astype(BF16) for k in range(4)
    ]


def kerr_term(fields, hot, weights_ref):
    size = fields.shape[0] // 2
    parts = jnp.concatenate(split(fields), axis=1)
    total = None
    for start in range(0, weights_ref.shape[1], TILE):
        here = slice(start, start + TILE)
        (lr, li), (mr, mi), (nr, ni) = (
            (y[:size], y[size:])
            for y in (dot(parts, jnp.concatenate([hot[k][:, here]] * 2, axis=0)) for k in (1, 2, 3))
        )
        weight = weights_ref[:, here]
        pr, pi = (lr * mr - li * mi, lr * mi + li * mr)
        pr, pi = (pr * weight, pi * weight)
        terms = jnp.concatenate([pr * ni - pi * nr, pr * nr + pi * ni], axis=0)
        terms = jnp.concatenate(split(terms), axis=1)
        added = lax.dot_general(
            terms,
            jnp.concatenate([hot[0][:, here]] * 2, axis=1),
            (((1,), (1,)), ((), ())),
            preferred_element_type=F32,
        )
        total = added if total is None else total + added
    return total


def kerr_kernel(last, x_ref, quartets_ref, weights_ref, *refs):
    modes = x_ref.shape[0] // 2
    linear = jnp.concatenate(
        [x_ref[pl.ds(ri, modes, stride=2), :].T for ri in range(2)], axis=0
    )
    hot = one_hots(quartets_ref, modes)
    first = kerr_term(linear, hot, weights_ref)
    second = kerr_term(linear + first, hot, weights_ref)
    updated = linear + 0.5 * (first + second)
    estimate = 0.5 * (second - first)
    sums = [jnp.sum(y * y, axis=0, keepdims=True) for y in (estimate, updated)]
    if not last:
        out_ref, sums_ref = refs
        for ri in range(2):
            out_ref[pl.ds(ri, modes, stride=2), :] = updated[ri * LANES : (ri + 1) * LANES].T
        sums_ref[0:1, :] = sums[0]
        sums_ref[1:2, :] = sums[1]
        return
    before_ref, out_ref, held_ref = refs
    for ri in range(2):
        held_ref[pl.ds(ri, modes, stride=2), :] = updated[ri * LANES : (ri + 1) * LANES].T
    norms = [before_ref[0:1, :], before_ref[1:2, :], *sums]
    shape = (modes // 4, modes)
    own = lax.broadcasted_iota(jnp.int32, shape, 1) // 4 == lax.broadcasted_iota(jnp.int32, shape, 0)
    picked = jnp.concatenate([jnp.where(own, norm, 0.0) for norm in norms], axis=1)
    shape = (4 * modes, LANES)
    source = lax.broadcasted_iota(jnp.int32, shape, 0)
    target = source // modes * 4 + source % 4
    moves = jnp.where(lax.broadcasted_iota(jnp.int32, shape, 1) == target, 1.0, 0.0).astype(BF16)
    high, low = split(picked)
    rows = dot(high, moves) + dot(low, moves)
    for group in range(modes // 4):
        out_ref[group * 9 : group * 9 + 8, :] = held_ref[group * 8 : group * 8 + 8, :]
        out_ref[group * 9 + 8 : group * 9 + 9, :] = rows[group : group + 1, :]


def regroup_kernel(x_ref, out_ref):
    norms = x_ref[8:9, :]
    for source in range(1, 32):
        norms = norms + x_ref[source * 9 + 8 : source * 9 + 9, :]
    for target in range(16):
        for half in range(2):
            source = target * 2 + half
            at = target * 17 + half * 8
            out_ref[at : at + 8, :] = x_ref[source * 9 : source * 9 + 8, :]
        out_ref[target * 17 + 16 : target * 17 + 17, :] = norms


def leave_kernel(x_ref, field_ref, errors_ref):
    norms = x_ref[16:17, :]
    for source in range(1, 16):
        norms = norms + x_ref[source * 17 + 16 : source * 17 + 17, :]
    size = pltpu.roll(norms, LANES - 4, 1)
    ratio = jnp.sqrt(norms / (size + EPSILON))
    errors_ref[0:1, :] = ratio[:, 0:4]
    errors_ref[1:2, :] = ratio[:, 8:12]
    for source in range(16):
        for half in range(2):
            tile = half * 16 + source
            for ri in range(2):
                field_ref[ri, :, tile * LANES : (tile + 1) * LANES] = x_ref[
                    pl.ds(source * 17 + half * 8 + ri, 4, stride=2), :
                ]


def rows_of(count):
    return jax.ShapeDtypeStruct((count, LANES), F32)


def exchange(array, axes, peers):
    rows = array.shape[0] // peers
    tile = 8 if rows % 8 == 0 else 1
    tiles = array.reshape(peers, rows // tile, tile, LANES)
    return lax.all_to_all(tiles, axes, 0, 0, tiled=True).reshape(array.shape)


def shards(field, beta, quartets, intersections):
    waves = jnp.asarray(host_waves())
    th, tl = (lax.axis_index(a).astype(jnp.int32)[None] for a in ("th", "tl"))
    weights = intersections.reshape(1, -1)
    along, across = (("th", "tl"), "mode")
    vmem = pl.BlockSpec(memory_space=pltpu.VMEM)
    smem = pl.BlockSpec(memory_space=pltpu.SMEM)
    limit = pltpu.CompilerParams(vmem_limit_bytes=16 * 1024 * 1024)

    def placed(kernel, state, *numbers):
        return pl.pallas_call(
            kernel,
            out_shape=rows_of(256),
            in_specs=[smem] * len(numbers) + [vmem],
            out_specs=vmem,
            compiler_params=limit,
        )(*numbers, state)

    def spectral(state):
        return pl.pallas_call(
            spectral_kernel,
            out_shape=rows_of(256),
            in_specs=[vmem] * 4,
            out_specs=vmem,
            compiler_params=limit,
        )(state, rotor, small, waves)

    square = jax.ShapeDtypeStruct((2, LANES, LANES), F32)
    rotor, small = pl.pallas_call(
        rotor_kernel,
        out_shape=(square, square),
        in_specs=[smem] * 3,
        out_specs=(vmem, vmem),
        compiler_params=limit,
    )(th, tl, beta)
    state = pl.pallas_call(
        enter_kernel,
        out_shape=rows_of(256),
        in_specs=[vmem, vmem],
        out_specs=vmem,
        compiler_params=limit,
    )(field, small)
    state = exchange(state, along, 16)
    state = placed(first_radix_kernel, state, tl)
    state = exchange(state, "tl", 4)
    norms = []
    for step in range(STEPS):
        last = step == STEPS - 1
        state = spectral(state)
        state = exchange(state, along, 16)
        state = placed(back_kernel, state, th, tl)
        state = exchange(state, across, 32)
        out = pl.pallas_call(
            functools.partial(kerr_kernel, last),
            out_shape=rows_of(288) if last else (rows_of(256), rows_of(8)),
            in_specs=[vmem] * (3 + len(norms)),
            out_specs=vmem if last else (vmem, vmem),
            scratch_shapes=[pltpu.VMEM((256, LANES), F32)] if last else [],
            compiler_params=limit,
        )(state, quartets, weights, *norms)
        if last:
            state = exchange(out, across, 32)
            break
        state, norm = out
        norms.append(norm)
        state = exchange(state, across, 32)
        state = placed(ahead_kernel, state, th, tl)
        state = exchange(state, along, 16)
    state = pl.pallas_call(
        regroup_kernel,
        out_shape=rows_of(272),
        in_specs=[vmem],
        out_specs=vmem,
        compiler_params=limit,
    )(state)
    state = exchange(state, along, 16)
    return pl.pallas_call(
        leave_kernel,
        out_shape=(
            jax.ShapeDtypeStruct(field.shape, F32),
            jax.ShapeDtypeStruct((STEPS, field.shape[1]), F32),
        ),
        in_specs=[vmem],
        out_specs=(vmem, vmem),
        compiler_params=limit,
    )(state)


def solution(mesh):
    finer = Mesh(mesh.devices.reshape(-1, 4, 4), ("mode", "th", "tl"))
    times = ("th", "tl")
    return jax.shard_map(
        shards,
        mesh=finer,
        in_specs=(P(None, "mode", times), P(None, "mode"), P(), P()),
        out_specs=(P(None, "mode", times), P(None, "mode")),
        check_vma=False,
    )
```

```python
import functools
import math

import jax
import jax.numpy as jnp
import ml_dtypes
import numpy as np
from jax import lax
from jax.experimental import pallas as pl
from jax.experimental.pallas import tpu as pltpu
from jax.sharding import Mesh
from jax.sharding import PartitionSpec as P

STEPS = 2
LANES = 128
HALF = 64
TIME = 65536
QUARTER = TIME // 4
TILE = 256
EPSILON = 1e-06
F32 = jnp.float32
BF16 = jnp.bfloat16


def two_parts(table):
    high = table.astype(ml_dtypes.bfloat16)
    low = (table - high.astype(np.float64)).astype(ml_dtypes.bfloat16)
    return np.stack([high, low])


@functools.cache
def host_waves():
    index = np.arange(LANES)
    wave = np.exp(-2j * math.pi / LANES * (index[:, None] * index[None, :] % LANES))
    ahead = np.block([[wave.real, -wave.imag], [wave.imag, wave.real]])
    back = np.block([[wave.real, wave.imag], [-wave.imag, wave.real]])

    tables = (ahead, ahead.T, back.T, back / TIME)
    return np.stack([two_parts(table) for table in tables])


def split(array):
    high = array.astype(BF16)
    return (high, (array - high.astype(F32)).astype(BF16))


def dot(left, right):
    return jnp.dot(left, right, preferred_element_type=F32)


def from_left(waves_ref, which, array):
    high, low = split(array)
    return dot(waves_ref[which, 0], high) + (
        dot(waves_ref[which, 0], low) + dot(waves_ref[which, 1], high)
    )


def from_right(array, waves_ref, which):
    high, low = split(array)
    return dot(high, waves_ref[which, 0]) + (
        dot(low, waves_ref[which, 0]) + dot(high, waves_ref[which, 1])
    )


def small_cosine_and_sine(x):
    z = x * x
    sine = ((-1.9515295891e-4 * z + 8.3321608736e-3) * z - 1.6666654611e-1) * z * x + x
    cosine = (
        (2.443315711809948e-5 * z - 1.388731625493765e-3) * z + 4.166664568298827e-2
    ) * z * z - 0.5 * z + 1.0
    return (cosine, sine)


def in_quarter(turns, cosine, sine):
    quarter = turns & 3
    odd = (quarter & 1) == 1
    c = jnp.where(odd, sine, cosine)
    s = jnp.where(odd, cosine, sine)
    c = jnp.where((quarter == 1) | (quarter == 2), -c, c)
    s = jnp.where(quarter >= 2, -s, s)
    return (c, s)


def cosine_and_sine(angle):
    scaled = angle * (2.0 / math.pi)
    turns = (scaled + jnp.where(scaled >= 0.0, 0.5, -0.5)).astype(jnp.int32)
    count = turns.astype(F32)
    x = angle - count * 1.5703125
    x = x - count * 4.837512969970703125e-4
    x = x - count * 7.5497899548918822e-8
    return in_quarter(turns, *small_cosine_and_sine(x))


def twist(number):
    turns = (number + TIME // 8) // QUARTER
    rest = (number - turns * QUARTER).astype(F32)
    return in_quarter(turns, *small_cosine_and_sine(rest * (2.0 * math.pi / TIME)))


def row_and_lane():
    return (lax.broadcasted_iota(jnp.int32, (8, LANES), axis) for axis in range(2))


def rotor_kernel(yx_ref, c_ref, th_ref, tl_ref, beta_ref, rotor_ref, small_ref):
    offset, slope, curve = (beta_ref[k, th_ref[0]] for k in range(3))
    shape = (LANES, LANES)
    row, lane = (lax.broadcasted_iota(jnp.int32, shape, axis) for axis in range(2))
    small_ref[0], small_ref[1] = twist(4 * row * lane)
    wave = 4 * (row + LANES * lane) + tl_ref[0]
    signed = jnp.where(wave < TIME // 2, wave, wave - TIME)
    frequency = signed.astype(F32) * (1.0 / (TIME / 2))
    angle = (
        math.pi * offset
        + 300.0 * slope * frequency
        + 3000.0 * curve * frequency * frequency
    )
    rotor_ref[0], rotor_ref[1] = cosine_and_sine(angle)


def enter_kernel(field_ref, after_ref, out_ref):
    for ri in range(2):
        for tile in range(32):
            zb, rest = (tile // 4 % 4, tile // 16 * 4 + tile % 4)
            out_ref[pl.ds(zb * 16 + ri * 8 + rest, 4, stride=64), :] = field_ref[
                ri, :, tile * LANES : (tile + 1) * LANES
            ]


def radix_ahead(x):
    (r0, i0), (r1, i1), (r2, i2), (r3, i3) = x
    sr, si, dr, di = r0 + r2, i0 + i2, r0 - r2, i0 - i2
    tr, ti, ur, ui = r1 + r3, i1 + i3, r1 - r3, i1 - i3
    return [(sr + tr, si + ti), (dr + ui, di - ur), (sr - tr, si - ti), (dr - ui, di + ur)]


def turned_back(pair, c, s):
    re, im = pair
    return (re * c + im * s, im * c - re * s)


def turned(pair, c, s):
    return turned_back(pair, c, -s)


def first_radix_kernel(zb_ref, x_ref, out_ref):
    row, lane = row_and_lane()
    place = (row // 4) * 2048 + (row % 4) * LANES + lane + zb_ref[0] * 512
    for v2 in range(4):
        at = [a * 64 + v2 * 16 for a in range(4)]
        y = radix_ahead([(x_ref[b : b + 8, :], x_ref[b + 8 : b + 16, :]) for b in at])
        for f in range(4):
            pair = turned_back(y[f], *twist(f * (place + v2 * 4096))) if f else y[f]
            for ri in range(2):
                for v0 in range(2):
                    first = f * 64 + ri * 8 + v2 * 2 + v0
                    out_ref[pl.ds(first, 4, stride=16), :] = pair[ri][v0 * 4 : v0 * 4 + 4]


def first_lanes(shape):
    return lax.broadcasted_iota(jnp.int32, shape, len(shape) - 1) < HALF


def swapped(array):
    return pltpu.roll(array, HALF, 1)


def times_i(array):
    moved = swapped(array)
    return jnp.where(first_lanes(array.shape), -moved, moved)


def middle_twists(yx_ref, th_ref, tl_ref):
    lane = lax.broadcasted_iota(jnp.int32, (1, LANES), 1)
    yx, w = (yx_ref[0], th_ref[0] * 4 + tl_ref[0])
    place = yx // 2 * 2048 + w * LANES + yx % 2 * HALF + lane % HALF
    return [None] + [twist(f * place) for f in range(1, 4)]


def back_kernel(yx_ref, c_ref, th_ref, tl_ref, x_ref, keep_ref, send_ref):
    twists = middle_twists(yx_ref, th_ref, tl_ref)
    y = [x_ref[pl.ds(f, HALF, stride=4), :] for f in range(4)]
    for f in range(1, 4):
        c, s = twists[f]
        y[f] = y[f] * c + times_i(y[f]) * s
    even, odd = (y[0] + y[2], y[1] + y[3])
    less, turn = (y[0] - y[2], times_i(y[1] - y[3]))
    x = [even + odd, less + turn, even - odd, less - turn]
    first = c_ref[0] == 0
    for low in range(2):
        rows = slice(low * HALF, low * HALF + HALF)
        keep_ref[rows, :] = jnp.where(first, x[low], x[low + 2])
        send_ref[rows, :] = jnp.where(first, x[low + 2], x[low])


def ahead_kernel(yx_ref, c_ref, th_ref, tl_ref, keep_ref, came_ref, out_ref):
    twists = middle_twists(yx_ref, th_ref, tl_ref)
    first = c_ref[0] == 0
    kept = [keep_ref[low * HALF : low * HALF + HALF, :] for low in range(2)]
    came = [came_ref[low * HALF : low * HALF + HALF, :] for low in range(2)]
    x = [jnp.where(first, k, m) for k, m in zip(kept, came)]
    x += [jnp.where(first, m, k) for k, m in zip(kept, came)]
    even, odd = (x[0] + x[2], x[1] + x[3])
    less, turn = (x[0] - x[2], times_i(x[1] - x[3]))
    y = [even + odd, less - turn, even - odd, less + turn]
    for f in range(4):
        if f:
            c, s = twists[f]
            y[f] = y[f] * c - times_i(y[f]) * s
        out_ref[pl.ds(f, HALF, stride=4), :] = y[f]


def spectral_kernel(from_tiles, x_ref, rotor_ref, small_ref, waves_ref, out_ref, held_ref):
    rotor = (rotor_ref[0], rotor_ref[1])
    small = (small_ref[0], small_ref[1])
    first = first_lanes((LANES, LANES))
    for tile in range(32):
        if from_tiles:
            w, ri = divmod(tile, 2)
            held_ref[pl.ds(ri * LANES + w, 8, stride=16), :] = x_ref[tile * 8 : tile * 8 + 8, :]
        elif tile < 16:
            v, half = divmod(tile, 2)
            at = half * LANES + v * 16
            held_ref[at : at + 16, :] = x_ref[tile * 16 : tile * 16 + 16, :]
    x = held_ref[...]
    if not from_tiles:
        low, high = (x[:LANES], x[LANES:])
        x = jnp.concatenate(
            [jnp.where(first, low, swapped(high)), jnp.where(first, swapped(low), high)], axis=0
        )
    y = from_left(waves_ref, 0, x)
    re, im = turned_back((y[:LANES], y[LANES:]), *small)
    y = from_right(jnp.concatenate([re, im], axis=1), waves_ref, 1)
    re, im = turned((y[:, :LANES], y[:, LANES:]), *rotor)
    y = from_right(jnp.concatenate([re, im], axis=1), waves_ref, 2)
    re, im = turned((y[:, :LANES], y[:, LANES:]), *small)
    y = from_left(waves_ref, 3, jnp.concatenate([re, im], axis=0))
    re, im = (y[:LANES], y[LANES:])
    halves = (jnp.where(first, re, swapped(im)), jnp.where(first, swapped(re), im))
    for v in range(8):
        for half in range(2):
            at = v * 32 + half * 16
            out_ref[at : at + 16, :] = halves[half][v * 16 : v * 16 + 16]


def one_hots(quartets_ref, modes):
    row = lax.broadcasted_iota(jnp.int32, (modes, 1), 0)
    half = modes // 2
    ids = row % half // 4 * 8 + row // half * 4 + row % 4
    return [
        jnp.where(quartets_ref[k : k + 1, :] == ids, 1.0, 0.0).astype(BF16) for k in range(4)
    ]


def kerr_term(fields, hot, weights_ref):
    size = fields.shape[0] // 2
    parts = jnp.concatenate(split(fields), axis=1)
    total = None
    for start in range(0, weights_ref.shape[1], TILE):
        here = slice(start, start + TILE)
        (lr, li), (mr, mi), (nr, ni) = (
            (y[:size], y[size:])
            for y in (dot(parts, jnp.concatenate([hot[k][:, here]] * 2, axis=0)) for k in (1, 2, 3))
        )
        weight = weights_ref[:, here]
        pr, pi = (lr * mr - li * mi, lr * mi + li * mr)
        pr, pi = (pr * weight, pi * weight)
        terms = jnp.concatenate([pr * ni - pi * nr, pr * nr + pi * ni], axis=0)
        terms = jnp.concatenate(split(terms), axis=1)
        added = lax.dot_general(
            terms,
            jnp.concatenate([hot[0][:, here]] * 2, axis=1),
            (((1,), (1,)), ((), ())),
            preferred_element_type=F32,
        )
        total = added if total is None else total + added
    return total


def kerr_kernel(last, c_ref, keep_ref, came_ref, quartets_ref, weights_ref, *refs):
    modes = keep_ref.shape[0]
    mine = c_ref[0] == 0
    blocks = []
    for low in range(2):
        rows = slice(low * HALF, low * HALF + HALF)
        kept, came = (keep_ref[rows, :], came_ref[rows, :])
        both = [jnp.where(mine, kept, came), jnp.where(mine, came, kept)]
        blocks.append(jnp.concatenate(both, axis=0).T)
    linear = jnp.concatenate([y[:HALF] for y in blocks] + [y[HALF:] for y in blocks], axis=0)
    hot = one_hots(quartets_ref, modes)
    first = kerr_term(linear, hot, weights_ref)
    second = kerr_term(linear + first, hot, weights_ref)
    updated = linear + 0.5 * (first + second)
    estimate = 0.5 * (second - first)
    sums = [jnp.sum(y * y, axis=0, keepdims=True) for y in (estimate, updated)]
    if not last:
        kept_ref, send_ref, sums_ref = refs
        for low in range(2):
            rows = slice(low * HALF, low * HALF + HALF)
            parts = [updated[ri * LANES + low * HALF :][:HALF] for ri in range(2)]
            both = jnp.concatenate(parts, axis=0).T
            kept_ref[rows, :] = jnp.where(mine, both[:HALF], both[HALF:])
            send_ref[rows, :] = jnp.where(mine, both[HALF:], both[:HALF])
        sums_ref[0:1, :] = sums[0]
        sums_ref[1:2, :] = sums[1]
        return
    before_ref, out_ref, held_ref = refs
    for ri in range(2):
        held_ref[pl.ds(ri, modes, stride=2), :] = updated[ri * LANES : (ri + 1) * LANES].T
    norms = [before_ref[0:1, :], before_ref[1:2, :], *sums]
    shape = (modes // 4, modes)
    own = lax.broadcasted_iota(jnp.int32, shape, 1) // 4 == lax.broadcasted_iota(jnp.int32, shape, 0)
    picked = jnp.concatenate([jnp.where(own, norm, 0.0) for norm in norms], axis=1)
    shape = (4 * modes, LANES)
    source = lax.broadcasted_iota(jnp.int32, shape, 0)
    target = source // modes * 4 + source % 4
    moves = jnp.where(lax.broadcasted_iota(jnp.int32, shape, 1) == target, 1.0, 0.0).astype(BF16)
    high, low = split(picked)
    rows = dot(high, moves) + dot(low, moves)
    for block in range(modes // 4):
        c, yx = divmod(block, 16)
        at = (yx * 2 + c) * 9
        out_ref[at : at + 8, :] = held_ref[block * 8 : block * 8 + 8, :]
        out_ref[at + 8 : at + 9, :] = rows[block : block + 1, :]


def regroup_kernel(x_ref, out_ref):
    norms = x_ref[8:9, :]
    for source in range(1, 32):
        norms = norms + x_ref[source * 9 + 8 : source * 9 + 9, :]
    first = first_lanes((8, LANES))
    for v in range(8):
        for c in range(2):
            at = [(v * 4 + half * 2 + c) * 9 for half in range(2)]
            low, high = (x_ref[b : b + 8, :] for b in at)
            made = (jnp.where(first, low, swapped(high)), jnp.where(first, swapped(low), high))
            for a in range(2):
                to = (c * 8 + a * 4 + v // 2) * 17 + v % 2 * 8
                out_ref[to : to + 8, :] = made[a]
    for target in range(16):
        out_ref[target * 17 + 16 : target * 17 + 17, :] = norms


def leave_kernel(x_ref, field_ref, errors_ref):
    norms = x_ref[16:17, :]
    for source in range(1, 16):
        norms = norms + x_ref[source * 17 + 16 : source * 17 + 17, :]
    size = pltpu.roll(norms, LANES - 4, 1)
    ratio = jnp.sqrt(norms / (size + EPSILON))
    errors_ref[0:1, :] = ratio[:, 0:4]
    errors_ref[1:2, :] = ratio[:, 8:12]
    for source in range(16):
        for half in range(2):
            tile = half * 16 + source
            for ri in range(2):
                field_ref[ri, :, tile * LANES : (tile + 1) * LANES] = x_ref[
                    pl.ds(source * 17 + half * 8 + ri, 4, stride=2), :
                ]


def rows_of(count):
    return jax.ShapeDtypeStruct((count, LANES), F32)


def exchange(array, axes, peers):
    rows = array.shape[0] // peers
    tile = 8 if rows % 8 == 0 else 1
    tiles = array.reshape(peers, rows // tile, tile, LANES)
    return lax.all_to_all(tiles, axes, 0, 0, tiled=True).reshape(array.shape)


def shards(field, beta, quartets, intersections):
    waves = jnp.asarray(host_waves())
    yx, c, th, tl = lax.optimization_barrier(
        tuple(lax.axis_index(a).astype(jnp.int32)[None] for a in ("yx", "c", "th", "tl"))
    )
    weights = intersections.reshape(1, -1)
    along, across, chips = (("th", "tl"), ("yx", "c"), ("yx", "th", "tl"))
    place = (yx, c, th, tl)
    vmem = pl.BlockSpec(memory_space=pltpu.VMEM)
    smem = pl.BlockSpec(memory_space=pltpu.SMEM)
    limit = pltpu.CompilerParams(vmem_limit_bytes=16 * 1024 * 1024)

    def placed(kernel, numbers, arrays, results):
        return pl.pallas_call(
            kernel,
            out_shape=results,
            in_specs=[smem] * len(numbers) + [vmem] * len(arrays),
            out_specs=tuple(vmem for _ in results) if isinstance(results, tuple) else vmem,
            compiler_params=limit,
        )(*numbers, *arrays)

    def other_core(array):
        return lax.ppermute(array, "c", [(0, 1), (1, 0)])

    def spectral(state, from_tiles):
        return pl.pallas_call(
            functools.partial(spectral_kernel, from_tiles),
            out_shape=rows_of(256),
            in_specs=[vmem] * 4,
            out_specs=vmem,
            scratch_shapes=[pltpu.VMEM((256, LANES), F32)],
            compiler_params=limit,
        )(state, rotor, small, waves)

    square = jax.ShapeDtypeStruct((2, LANES, LANES), F32)
    rotor, small = pl.pallas_call(
        rotor_kernel,
        out_shape=(square, square),
        in_specs=[smem] * 5,
        out_specs=(vmem, vmem),
        compiler_params=limit,
    )(*place, beta)
    state = pl.pallas_call(
        enter_kernel,
        out_shape=rows_of(256),
        in_specs=[vmem, vmem],
        out_specs=vmem,
        compiler_params=limit,
    )(field, small)
    state = exchange(state, along, 16)
    state = placed(first_radix_kernel, (tl,), (state,), rows_of(256))
    state = exchange(state, "tl", 4)
    pair = (rows_of(128), rows_of(128))
    norms = []
    for step in range(STEPS):
        last = step == STEPS - 1
        state = spectral(state, step == 0)
        state = exchange(state, chips, 256)
        keep, send = placed(back_kernel, place, (state,), pair)
        came = other_core(send)
        out = pl.pallas_call(
            functools.partial(kerr_kernel, last),
            out_shape=rows_of(288) if last else (*pair, rows_of(8)),
            in_specs=[smem] + [vmem] * (4 + len(norms)),
            out_specs=vmem if last else (vmem, vmem, vmem),
            scratch_shapes=[pltpu.VMEM((256, LANES), F32)] if last else [],
            compiler_params=limit,
        )(c, keep, came, quartets, weights, *norms)
        if last:
            state = exchange(out, across, 32)
            break
        keep, send, norm = out
        norms.append(norm)
        state = placed(ahead_kernel, place, (keep, other_core(send)), rows_of(256))
        state = exchange(state, chips, 256)
    state = pl.pallas_call(
        regroup_kernel,
        out_shape=rows_of(272),
        in_specs=[vmem],
        out_specs=vmem,
        compiler_params=limit,
    )(state)
    state = exchange(state, along, 16)
    return pl.pallas_call(
        leave_kernel,
        out_shape=(
            jax.ShapeDtypeStruct(field.shape, F32),
            jax.ShapeDtypeStruct((STEPS, field.shape[1]), F32),
        ),
        in_specs=[vmem],
        out_specs=(vmem, vmem),
        compiler_params=limit,
    )(state)


def solution(mesh):
    finer = Mesh(mesh.devices.reshape(-1, 2, 4, 4), ("yx", "c", "th", "tl"))
    modes, times = (("yx", "c"), ("th", "tl"))
    return jax.shard_map(
        shards,
        mesh=finer,
        in_specs=(P(None, modes, times), P(None, modes), P(), P()),
        out_specs=(P(None, modes, times), P(None, modes)),
        check_vma=False,
    )
```

```python
import functools
import math

import jax
import jax.numpy as jnp
import ml_dtypes
import numpy as np
from jax import lax
from jax.experimental import pallas as pl
from jax.experimental.pallas import tpu as pltpu
from jax.sharding import Mesh
from jax.sharding import PartitionSpec as P

STEPS = 2
LANES = 128
TIME = 65536
QUARTER = TIME // 4
TILE = 256
EPSILON = 1e-06
F32 = jnp.float32
BF16 = jnp.bfloat16


def two_parts(table):
    high = table.astype(ml_dtypes.bfloat16)
    low = (table - high.astype(np.float64)).astype(ml_dtypes.bfloat16)
    return np.stack([high, low])


@functools.cache
def host_waves():
    index = np.arange(LANES)
    wave = np.exp(-2j * math.pi / LANES * (index[:, None] * index[None, :] % LANES))
    ahead = np.block([[wave.real, -wave.imag], [wave.imag, wave.real]])
    back = np.block([[wave.real, wave.imag], [-wave.imag, wave.real]])

    def row_order(place):
        return np.array([ri * LANES + p for p, ri in place])

    tile_order = row_order(
        [(v * 16 + w, ri) for w in range(16) for ri in range(2) for v in range(8)]
    )
    tables = (ahead[:, tile_order], ahead.T, back.T, back[tile_order] / TIME)
    return np.stack([two_parts(table) for table in tables])


def split(array):
    high = array.astype(BF16)
    return (high, (array - high.astype(F32)).astype(BF16))


def dot(left, right):
    return jnp.dot(left, right, preferred_element_type=F32)


def from_left(waves_ref, which, array):
    high, low = split(array)
    return dot(waves_ref[which, 0], high) + (
        dot(waves_ref[which, 0], low) + dot(waves_ref[which, 1], high)
    )


def from_right(array, waves_ref, which):
    high, low = split(array)
    return dot(high, waves_ref[which, 0]) + (
        dot(low, waves_ref[which, 0]) + dot(high, waves_ref[which, 1])
    )


def small_cosine_and_sine(x):
    z = x * x
    sine = ((-1.9515295891e-4 * z + 8.3321608736e-3) * z - 1.6666654611e-1) * z * x + x
    cosine = (
        (2.443315711809948e-5 * z - 1.388731625493765e-3) * z + 4.166664568298827e-2
    ) * z * z - 0.5 * z + 1.0
    return (cosine, sine)


def in_quarter(turns, cosine, sine):
    quarter = turns & 3
    odd = (quarter & 1) == 1
    c = jnp.where(odd, sine, cosine)
    s = jnp.where(odd, cosine, sine)
    c = jnp.where((quarter == 1) | (quarter == 2), -c, c)
    s = jnp.where(quarter >= 2, -s, s)
    return (c, s)


def cosine_and_sine(angle):
    scaled = angle * (2.0 / math.pi)
    turns = (scaled + jnp.where(scaled >= 0.0, 0.5, -0.5)).astype(jnp.int32)
    count = turns.astype(F32)
    x = angle - count * 1.5703125
    x = x - count * 4.837512969970703125e-4
    x = x - count * 7.5497899548918822e-8
    return in_quarter(turns, *small_cosine_and_sine(x))


def twist(number):
    turns = (number + TIME // 8) >> 14
    rest = (number - (turns << 14)).astype(F32)
    return in_quarter(turns, *small_cosine_and_sine(rest * (2.0 * math.pi / TIME)))


def row_and_lane():
    return (lax.broadcasted_iota(jnp.int32, (8, LANES), axis) for axis in range(2))


def small_kernel(th_ref, small_ref):
    row, lane = (lax.broadcasted_iota(jnp.int32, (LANES, LANES), axis) for axis in range(2))
    small_ref[0], small_ref[1] = twist(4 * row * lane)


def rotor_kernel(th_ref, tl_ref, beta_ref, after_ref, rotor_ref):
    offset, slope, curve = (beta_ref[k, th_ref[0]] for k in range(3))
    row, lane = (lax.broadcasted_iota(jnp.int32, (LANES, LANES), axis) for axis in range(2))
    wave = 4 * (row + LANES * lane) + tl_ref[0]
    signed = jnp.where(wave < TIME // 2, wave, wave - TIME)
    frequency = signed.astype(F32) * (1.0 / (TIME / 2))
    angle = (
        math.pi * offset
        + 300.0 * slope * frequency
        + 3000.0 * curve * frequency * frequency
    )
    rotor_ref[0], rotor_ref[1] = cosine_and_sine(angle)


def enter_kernel(field_ref, after_ref, out_ref):
    for ri in range(2):
        for tile in range(32):
            zb, rest = (tile // 4 % 4, tile // 16 * 4 + tile % 4)
            out_ref[pl.ds(zb * 16 + ri * 8 + rest, 4, stride=64), :] = field_ref[
                ri, :, tile * LANES : (tile + 1) * LANES
            ]


def radix_ahead(x):
    (r0, i0), (r1, i1), (r2, i2), (r3, i3) = x
    sr, si, dr, di = r0 + r2, i0 + i2, r0 - r2, i0 - i2
    tr, ti, ur, ui = r1 + r3, i1 + i3, r1 - r3, i1 - i3
    return [(sr + tr, si + ti), (dr + ui, di - ur), (sr - tr, si - ti), (dr - ui, di + ur)]


def radix_back(x):
    out = radix_ahead(x)
    return [out[0], out[3], out[2], out[1]]


def turned_back(pair, c, s):
    re, im = pair
    return (re * c + im * s, im * c - re * s)


def turned(pair, c, s):
    return turned_back(pair, c, -s)


def first_radix_kernel(zb_ref, x_ref, out_ref):
    row, lane = row_and_lane()
    place = (row // 4) * 2048 + (row % 4) * LANES + lane + zb_ref[0] * 512
    for v2 in range(4):
        at = [a * 64 + v2 * 16 for a in range(4)]
        y = radix_ahead([(x_ref[b : b + 8, :], x_ref[b + 8 : b + 16, :]) for b in at])
        for f in range(4):
            pair = turned_back(y[f], *twist(f * (place + v2 * 4096))) if f else y[f]
            for ri in range(2):
                for v0 in range(2):
                    first = f * 64 + ri * 8 + v2 * 2 + v0
                    out_ref[pl.ds(first, 4, stride=16), :] = pair[ri][v0 * 4 : v0 * 4 + 4]


def middle_twists(th_ref, tl_ref):
    row, lane = row_and_lane()
    place = row * 2048 + lane + (th_ref[0] * 4 + tl_ref[0]) * LANES
    return [None] + [twist(f * place) for f in range(1, 4)]


def ahead_kernel(th_ref, tl_ref, x_ref, out_ref):
    twists = middle_twists(th_ref, tl_ref)
    for low in range(4):
        y = radix_ahead(
            [
                tuple(x_ref[pl.ds(a * 64 + low * 2 + ri, 8, stride=8), :] for ri in range(2))
                for a in range(4)
            ]
        )
        for f in range(4):
            re, im = turned_back(y[f], *twists[f]) if f else y[f]
            at = low * 64 + f * 16
            out_ref[at : at + 8, :] = re
            out_ref[at + 8 : at + 16, :] = im


def back_kernel(th_ref, tl_ref, x_ref, out_ref):
    twists = middle_twists(th_ref, tl_ref)
    for low in range(4):
        y = []
        for f in range(4):
            at = low * 64 + f * 16
            pair = (x_ref[at : at + 8, :], x_ref[at + 8 : at + 16, :])
            y.append(turned(pair, *twists[f]) if f else pair)
        for a, pair in enumerate(radix_back(y)):
            for ri in range(2):
                out_ref[pl.ds(a * 64 + low * 2 + ri, 8, stride=8), :] = pair[ri]


def spectral_kernel(x_ref, rotor_ref, small_ref, waves_ref, out_ref):
    rotor = (rotor_ref[0], rotor_ref[1])
    small = (small_ref[0], small_ref[1])
    y = from_left(waves_ref, 0, x_ref[...])
    re, im = turned_back((y[:LANES], y[LANES:]), *small)
    y = from_right(jnp.concatenate([re, im], axis=1), waves_ref, 1)
    re, im = turned((y[:, :LANES], y[:, LANES:]), *rotor)
    y = from_right(jnp.concatenate([re, im], axis=1), waves_ref, 2)
    re, im = turned((y[:, :LANES], y[:, LANES:]), *small)
    out_ref[...] = from_left(waves_ref, 3, jnp.concatenate([re, im], axis=0))


def one_hots(quartets_ref, modes):
    ids = lax.broadcasted_iota(jnp.int32, (modes, quartets_ref.shape[1]), 0)
    return [
        jnp.where(quartets_ref[k : k + 1, :] == ids, 1.0, 0.0).astype(BF16) for k in range(4)
    ]


def kerr_term(fields, hot, weights_ref):
    size = fields.shape[0] // 2
    parts = jnp.concatenate(split(fields), axis=1)
    total = None
    for start in range(0, weights_ref.shape[1], TILE):
        here = slice(start, start + TILE)
        (lr, li), (mr, mi), (nr, ni) = (
            (y[:size], y[size:])
            for y in (dot(parts, jnp.concatenate([hot[k][:, here]] * 2, axis=0)) for k in (1, 2, 3))
        )
        weight = weights_ref[:, here]
        pr, pi = (lr * mr - li * mi, lr * mi + li * mr)
        pr, pi = (pr * weight, pi * weight)
        terms = jnp.concatenate([pr * ni - pi * nr, pr * nr + pi * ni], axis=0)
        terms = jnp.concatenate(split(terms), axis=1)
        added = lax.dot_general(
            terms,
            jnp.concatenate([hot[0][:, here]] * 2, axis=1),
            (((1,), (1,)), ((), ())),
            preferred_element_type=F32,
        )
        total = added if total is None else total + added
    return total


def kerr_kernel(last, x_ref, quartets_ref, weights_ref, *refs):
    modes = x_ref.shape[0] // 2
    linear = jnp.concatenate(
        [x_ref[pl.ds(ri, modes, stride=2), :].T for ri in range(2)], axis=0
    )
    hot = one_hots(quartets_ref, modes)
    first = kerr_term(linear, hot, weights_ref)
    second = kerr_term(linear + first, hot, weights_ref)
    updated = linear + 0.5 * (first + second)
    estimate = 0.5 * (second - first)
    sums = [jnp.sum(y * y, axis=0, keepdims=True) for y in (estimate, updated)]
    if not last:
        out_ref, sums_ref = refs
        for ri in range(2):
            out_ref[pl.ds(ri, modes, stride=2), :] = updated[ri * LANES : (ri + 1) * LANES].T
        sums_ref[0:1, :] = sums[0]
        sums_ref[1:2, :] = sums[1]
        return
    before_ref, out_ref, held_ref = refs
    for ri in range(2):
        held_ref[pl.ds(ri, modes, stride=2), :] = updated[ri * LANES : (ri + 1) * LANES].T
    norms = [before_ref[0:1, :], before_ref[1:2, :], *sums]
    shape = (modes // 4, modes)
    own = lax.broadcasted_iota(jnp.int32, shape, 1) // 4 == lax.broadcasted_iota(jnp.int32, shape, 0)
    picked = jnp.concatenate([jnp.where(own, norm, 0.0) for norm in norms], axis=1)
    shape = (4 * modes, LANES)
    source = lax.broadcasted_iota(jnp.int32, shape, 0)
    target = source // modes * 4 + source % 4
    moves = jnp.where(lax.broadcasted_iota(jnp.int32, shape, 1) == target, 1.0, 0.0).astype(BF16)
    high, low = split(picked)
    rows = dot(high, moves) + dot(low, moves)
    for group in range(modes // 4):
        out_ref[group * 9 : group * 9 + 8, :] = held_ref[group * 8 : group * 8 + 8, :]
        out_ref[group * 9 + 8 : group * 9 + 9, :] = rows[group : group + 1, :]


def regroup_kernel(x_ref, out_ref):
    norms = x_ref[8:9, :]
    for source in range(1, 32):
        norms = norms + x_ref[source * 9 + 8 : source * 9 + 9, :]
    for target in range(16):
        for half in range(2):
            source = target * 2 + half
            at = target * 17 + half * 8
            out_ref[at : at + 8, :] = x_ref[source * 9 : source * 9 + 8, :]
        out_ref[target * 17 + 16 : target * 17 + 17, :] = norms


def leave_kernel(x_ref, field_ref, errors_ref):
    norms = x_ref[16:17, :]
    for source in range(1, 16):
        norms = norms + x_ref[source * 17 + 16 : source * 17 + 17, :]
    size = pltpu.roll(norms, LANES - 4, 1)
    ratio = jnp.sqrt(norms / (size + EPSILON))
    errors_ref[0:1, :] = ratio[:, 0:4]
    errors_ref[1:2, :] = ratio[:, 8:12]
    for source in range(16):
        for half in range(2):
            tile = half * 16 + source
            for ri in range(2):
                field_ref[ri, :, tile * LANES : (tile + 1) * LANES] = x_ref[
                    pl.ds(source * 17 + half * 8 + ri, 4, stride=2), :
                ]


def rows_of(count):
    return jax.ShapeDtypeStruct((count, LANES), F32)


def exchange(array, axes, peers):
    rows = array.shape[0] // peers
    tile = 8 if rows % 8 == 0 else 1
    tiles = array.reshape(peers, rows // tile, tile, LANES)
    return lax.all_to_all(tiles, axes, 0, 0, tiled=True).reshape(array.shape)


def shards(field, beta, quartets, intersections):
    waves = jnp.asarray(host_waves())
    th, tl = (lax.axis_index(a).astype(jnp.int32)[None] for a in ("th", "tl"))
    weights = intersections.reshape(1, -1)
    along, across = (("th", "tl"), "mode")
    vmem = pl.BlockSpec(memory_space=pltpu.VMEM)
    smem = pl.BlockSpec(memory_space=pltpu.SMEM)
    limit = pltpu.CompilerParams(vmem_limit_bytes=16 * 1024 * 1024)

    def placed(kernel, state, *numbers):
        return pl.pallas_call(
            kernel,
            out_shape=rows_of(256),
            in_specs=[smem] * len(numbers) + [vmem],
            out_specs=vmem,
            compiler_params=limit,
        )(*numbers, state)

    def spectral(state):
        return pl.pallas_call(
            spectral_kernel,
            out_shape=rows_of(256),
            in_specs=[vmem] * 4,
            out_specs=vmem,
            compiler_params=limit,
        )(state, rotor, small, waves)

    square = jax.ShapeDtypeStruct((2, LANES, LANES), F32)
    cost = pl.CostEstimate(flops=4 * 10**8, bytes_accessed=2 * TIME, transcendentals=0)
    small = pl.pallas_call(
        small_kernel,
        out_shape=square,
        in_specs=[smem],
        out_specs=vmem,
        compiler_params=limit,
        cost_estimate=cost,
    )(th)
    rotor = pl.pallas_call(
        rotor_kernel,
        out_shape=square,
        in_specs=[smem] * 3 + [vmem],
        out_specs=vmem,
        compiler_params=limit,
        cost_estimate=cost,
    )(th, tl, beta, small)
    state = pl.pallas_call(
        enter_kernel,
        out_shape=rows_of(256),
        in_specs=[vmem, vmem],
        out_specs=vmem,
        compiler_params=limit,
    )(field, rotor)
    state = exchange(state, along, 16)
    state = placed(first_radix_kernel, state, tl)
    state = exchange(state, "tl", 4)
    norms = []
    for step in range(STEPS):
        last = step == STEPS - 1
        state = spectral(state)
        state = exchange(state, along, 16)
        state = placed(back_kernel, state, th, tl)
        state = exchange(state, across, 32)
        out = pl.pallas_call(
            functools.partial(kerr_kernel, last),
            out_shape=rows_of(288) if last else (rows_of(256), rows_of(8)),
            in_specs=[vmem] * (3 + len(norms)),
            out_specs=vmem if last else (vmem, vmem),
            scratch_shapes=[pltpu.VMEM((256, LANES), F32)] if last else [],
            compiler_params=limit,
        )(state, quartets, weights, *norms)
        if last:
            state = exchange(out, across, 32)
            break
        state, norm = out
        norms.append(norm)
        state = exchange(state, across, 32)
        state = placed(ahead_kernel, state, th, tl)
        state = exchange(state, along, 16)
    state = pl.pallas_call(
        regroup_kernel,
        out_shape=rows_of(272),
        in_specs=[vmem],
        out_specs=vmem,
        compiler_params=limit,
    )(state)
    state = exchange(state, along, 16)
    return pl.pallas_call(
        leave_kernel,
        out_shape=(
            jax.ShapeDtypeStruct(field.shape, F32),
            jax.ShapeDtypeStruct((STEPS, field.shape[1]), F32),
        ),
        in_specs=[vmem],
        out_specs=(vmem, vmem),
        compiler_params=limit,
    )(state)


def solution(mesh):
    finer = Mesh(mesh.devices.reshape(-1, 4, 4), ("mode", "th", "tl"))
    times = ("th", "tl")
    return jax.shard_map(
        shards,
        mesh=finer,
        in_specs=(P(None, "mode", times), P(None, "mode"), P(), P()),
        out_specs=(P(None, "mode", times), P(None, "mode")),
        check_vma=False,
    )
```

```python
import functools
import math

import jax
import jax.numpy as jnp
import ml_dtypes
import numpy as np
from jax import lax
from jax.experimental import pallas as pl
from jax.experimental.pallas import tpu as pltpu
from jax.sharding import Mesh
from jax.sharding import PartitionSpec as P

STEPS = 2
LANES = 128
TIME = 65536
QUARTER = TIME // 4
TILE = 256
EPSILON = 1e-06
F32 = jnp.float32
BF16 = jnp.bfloat16


def two_parts(table):
    high = table.astype(ml_dtypes.bfloat16)
    low = (table - high.astype(np.float64)).astype(ml_dtypes.bfloat16)
    return np.stack([high, low])


@functools.cache
def host_waves():
    index = np.arange(LANES)
    wave = np.exp(-2j * math.pi / LANES * (index[:, None] * index[None, :] % LANES))
    ahead = np.block([[wave.real, -wave.imag], [wave.imag, wave.real]])
    back = np.block([[wave.real, wave.imag], [-wave.imag, wave.real]])

    def row_order(place):
        return np.array([ri * LANES + p for p, ri in place])

    tile_order = row_order(
        [(v * 16 + w, ri) for w in range(16) for ri in range(2) for v in range(8)]
    )
    tables = (ahead[:, tile_order], ahead.T, back.T, back[tile_order] / TIME)
    return np.stack([two_parts(table) for table in tables])


def split(array):
    high = array.astype(BF16)
    return (high, (array - high.astype(F32)).astype(BF16))


def dot(left, right):
    return jnp.dot(left, right, preferred_element_type=F32)


def from_left(waves_ref, which, array):
    high, low = split(array)
    return dot(waves_ref[which, 0], high) + (
        dot(waves_ref[which, 0], low) + dot(waves_ref[which, 1], high)
    )


def from_right(array, waves_ref, which):
    high, low = split(array)
    return dot(high, waves_ref[which, 0]) + (
        dot(low, waves_ref[which, 0]) + dot(high, waves_ref[which, 1])
    )


def small_cosine_and_sine(x):
    z = x * x
    sine = ((-1.9515295891e-4 * z + 8.3321608736e-3) * z - 1.6666654611e-1) * z * x + x
    cosine = (
        (2.443315711809948e-5 * z - 1.388731625493765e-3) * z + 4.166664568298827e-2
    ) * z * z - 0.5 * z + 1.0
    return (cosine, sine)


def in_quarter(turns, cosine, sine):
    quarter = turns & 3
    odd = (quarter & 1) == 1
    c = jnp.where(odd, sine, cosine)
    s = jnp.where(odd, cosine, sine)
    c = jnp.where((quarter == 1) | (quarter == 2), -c, c)
    s = jnp.where(quarter >= 2, -s, s)
    return (c, s)


def cosine_and_sine(angle):
    scaled = angle * (2.0 / math.pi)
    turns = (scaled + jnp.where(scaled >= 0.0, 0.5, -0.5)).astype(jnp.int32)
    count = turns.astype(F32)
    x = angle - count * 1.5703125
    x = x - count * 4.837512969970703125e-4
    x = x - count * 7.5497899548918822e-8
    return in_quarter(turns, *small_cosine_and_sine(x))


def twist(number):
    turns = (number + TIME // 8) >> 14
    rest = (number - (turns << 14)).astype(F32)
    return in_quarter(turns, *small_cosine_and_sine(rest * (2.0 * math.pi / TIME)))


def row_and_lane():
    return (lax.broadcasted_iota(jnp.int32, (8, LANES), axis) for axis in range(2))


def small_kernel(th_ref, small_ref):
    row, lane = (lax.broadcasted_iota(jnp.int32, (LANES, LANES), axis) for axis in range(2))
    small_ref[0], small_ref[1] = twist(4 * row * lane)


def rotor_kernel(th_ref, tl_ref, beta_ref, after_ref, rotor_ref):
    own = lax.broadcasted_iota(jnp.int32, beta_ref.shape, 1) == th_ref[0]
    beta = jnp.sum(jnp.where(own, beta_ref[...], 0.0), axis=1, keepdims=True)
    offset, slope, curve = (beta[k : k + 1, :] for k in range(3))
    row, lane = (lax.broadcasted_iota(jnp.int32, (LANES, LANES), axis) for axis in range(2))
    wave = 4 * (row + LANES * lane) + tl_ref[0]
    signed = jnp.where(wave < TIME // 2, wave, wave - TIME)
    frequency = signed.astype(F32) * (1.0 / (TIME / 2))
    angle = (
        math.pi * offset
        + 300.0 * slope * frequency
        + 3000.0 * curve * frequency * frequency
    )
    rotor_ref[0], rotor_ref[1] = cosine_and_sine(angle)


def enter_kernel(field_ref, after_ref, out_ref):
    for ri in range(2):
        for tile in range(32):
            zb, rest = (tile // 4 % 4, tile // 16 * 4 + tile % 4)
            out_ref[pl.ds(zb * 16 + ri * 8 + rest, 4, stride=64), :] = field_ref[
                ri, :, tile * LANES : (tile + 1) * LANES
            ]


def radix_ahead(x):
    (r0, i0), (r1, i1), (r2, i2), (r3, i3) = x
    sr, si, dr, di = r0 + r2, i0 + i2, r0 - r2, i0 - i2
    tr, ti, ur, ui = r1 + r3, i1 + i3, r1 - r3, i1 - i3
    return [(sr + tr, si + ti), (dr + ui, di - ur), (sr - tr, si - ti), (dr - ui, di + ur)]


def radix_back(x):
    out = radix_ahead(x)
    return [out[0], out[3], out[2], out[1]]


def turned_back(pair, c, s):
    re, im = pair
    return (re * c + im * s, im * c - re * s)


def turned(pair, c, s):
    return turned_back(pair, c, -s)


def first_radix_kernel(zb_ref, x_ref, out_ref):
    row, lane = row_and_lane()
    place = (row // 4) * 2048 + (row % 4) * LANES + lane + zb_ref[0] * 512
    for v2 in range(4):
        at = [a * 64 + v2 * 16 for a in range(4)]
        y = radix_ahead([(x_ref[b : b + 8, :], x_ref[b + 8 : b + 16, :]) for b in at])
        for f in range(4):
            pair = turned_back(y[f], *twist(f * (place + v2 * 4096))) if f else y[f]
            for ri in range(2):
                for v0 in range(2):
                    first = f * 64 + ri * 8 + v2 * 2 + v0
                    out_ref[pl.ds(first, 4, stride=16), :] = pair[ri][v0 * 4 : v0 * 4 + 4]


def middle_twists(th_ref, tl_ref):
    row, lane = row_and_lane()
    place = row * 2048 + lane + (th_ref[0] * 4 + tl_ref[0]) * LANES
    return [None] + [twist(f * place) for f in range(1, 4)]


def ahead_kernel(th_ref, tl_ref, x_ref, out_ref):
    twists = middle_twists(th_ref, tl_ref)
    for low in range(4):
        y = radix_ahead(
            [
                tuple(x_ref[pl.ds(a * 64 + low * 2 + ri, 8, stride=8), :] for ri in range(2))
                for a in range(4)
            ]
        )
        for f in range(4):
            re, im = turned_back(y[f], *twists[f]) if f else y[f]
            at = low * 64 + f * 16
            out_ref[at : at + 8, :] = re
            out_ref[at + 8 : at + 16, :] = im


def back_kernel(th_ref, tl_ref, x_ref, out_ref):
    twists = middle_twists(th_ref, tl_ref)
    for low in range(4):
        y = []
        for f in range(4):
            at = low * 64 + f * 16
            pair = (x_ref[at : at + 8, :], x_ref[at + 8 : at + 16, :])
            y.append(turned(pair, *twists[f]) if f else pair)
        for a, pair in enumerate(radix_back(y)):
            for ri in range(2):
                out_ref[pl.ds(a * 64 + low * 2 + ri, 8, stride=8), :] = pair[ri]


def spectral_kernel(x_ref, rotor_ref, small_ref, waves_ref, out_ref):
    rotor = (rotor_ref[0], rotor_ref[1])
    small = (small_ref[0], small_ref[1])
    y = from_left(waves_ref, 0, x_ref[...])
    re, im = turned_back((y[:LANES], y[LANES:]), *small)
    y = from_right(jnp.concatenate([re, im], axis=1), waves_ref, 1)
    re, im = turned((y[:, :LANES], y[:, LANES:]), *rotor)
    y = from_right(jnp.concatenate([re, im], axis=1), waves_ref, 2)
    re, im = turned((y[:, :LANES], y[:, LANES:]), *small)
    out_ref[...] = from_left(waves_ref, 3, jnp.concatenate([re, im], axis=0))


def one_hots(quartets_ref, modes):
    ids = lax.broadcasted_iota(jnp.int32, (modes, quartets_ref.shape[1]), 0)
    return [
        jnp.where(quartets_ref[k : k + 1, :] == ids, 1.0, 0.0).astype(BF16) for k in range(4)
    ]


def kerr_term(fields, hot, weights_ref):
    size = fields.shape[0] // 2
    parts = jnp.concatenate(split(fields), axis=1)
    total = None
    for start in range(0, weights_ref.shape[1], TILE):
        here = slice(start, start + TILE)
        (lr, li), (mr, mi), (nr, ni) = (
            (y[:size], y[size:])
            for y in (dot(parts, jnp.concatenate([hot[k][:, here]] * 2, axis=0)) for k in (1, 2, 3))
        )
        weight = weights_ref[:, here]
        pr, pi = (lr * mr - li * mi, lr * mi + li * mr)
        pr, pi = (pr * weight, pi * weight)
        terms = jnp.concatenate([pr * ni - pi * nr, pr * nr + pi * ni], axis=0)
        terms = jnp.concatenate(split(terms), axis=1)
        added = lax.dot_general(
            terms,
            jnp.concatenate([hot[0][:, here]] * 2, axis=1),
            (((1,), (1,)), ((), ())),
            preferred_element_type=F32,
        )
        total = added if total is None else total + added
    return total


def kerr_kernel(last, x_ref, quartets_ref, weights_ref, *refs):
    modes = x_ref.shape[0] // 2
    linear = jnp.concatenate(
        [x_ref[pl.ds(ri, modes, stride=2), :].T for ri in range(2)], axis=0
    )
    hot = one_hots(quartets_ref, modes)
    first = kerr_term(linear, hot, weights_ref)
    second = kerr_term(linear + first, hot, weights_ref)
    updated = linear + 0.5 * (first + second)
    estimate = 0.5 * (second - first)
    sums = [jnp.sum(y * y, axis=0, keepdims=True) for y in (estimate, updated)]
    if not last:
        out_ref, sums_ref = refs
        for ri in range(2):
            out_ref[pl.ds(ri, modes, stride=2), :] = updated[ri * LANES : (ri + 1) * LANES].T
        sums_ref[0:1, :] = sums[0]
        sums_ref[1:2, :] = sums[1]
        return
    before_ref, out_ref, held_ref = refs
    for ri in range(2):
        held_ref[pl.ds(ri, modes, stride=2), :] = updated[ri * LANES : (ri + 1) * LANES].T
    norms = [before_ref[0:1, :], before_ref[1:2, :], *sums]
    shape = (modes // 4, modes)
    own = lax.broadcasted_iota(jnp.int32, shape, 1) // 4 == lax.broadcasted_iota(jnp.int32, shape, 0)
    picked = jnp.concatenate([jnp.where(own, norm, 0.0) for norm in norms], axis=1)
    shape = (4 * modes, LANES)
    source = lax.broadcasted_iota(jnp.int32, shape, 0)
    target = source // modes * 4 + source % 4
    moves = jnp.where(lax.broadcasted_iota(jnp.int32, shape, 1) == target, 1.0, 0.0).astype(BF16)
    high, low = split(picked)
    rows = dot(high, moves) + dot(low, moves)
    for group in range(modes // 4):
        out_ref[group * 9 : group * 9 + 8, :] = held_ref[group * 8 : group * 8 + 8, :]
        out_ref[group * 9 + 8 : group * 9 + 9, :] = rows[group : group + 1, :]


def regroup_kernel(x_ref, out_ref):
    norms = x_ref[8:9, :]
    for source in range(1, 32):
        norms = norms + x_ref[source * 9 + 8 : source * 9 + 9, :]
    for target in range(16):
        for half in range(2):
            source = target * 2 + half
            at = target * 17 + half * 8
            out_ref[at : at + 8, :] = x_ref[source * 9 : source * 9 + 8, :]
        out_ref[target * 17 + 16 : target * 17 + 17, :] = norms


def leave_kernel(x_ref, field_ref, errors_ref):
    norms = x_ref[16:17, :]
    for source in range(1, 16):
        norms = norms + x_ref[source * 17 + 16 : source * 17 + 17, :]
    size = pltpu.roll(norms, LANES - 4, 1)
    ratio = jnp.sqrt(norms / (size + EPSILON))
    errors_ref[0:1, :] = ratio[:, 0:4]
    errors_ref[1:2, :] = ratio[:, 8:12]
    for source in range(16):
        for half in range(2):
            tile = half * 16 + source
            for ri in range(2):
                field_ref[ri, :, tile * LANES : (tile + 1) * LANES] = x_ref[
                    pl.ds(source * 17 + half * 8 + ri, 4, stride=2), :
                ]


def rows_of(count):
    return jax.ShapeDtypeStruct((count, LANES), F32)


def exchange(array, axes, peers):
    rows = array.shape[0] // peers
    tile = 8 if rows % 8 == 0 else 1
    tiles = array.reshape(peers, rows // tile, tile, LANES)
    return lax.all_to_all(tiles, axes, 0, 0, tiled=True).reshape(array.shape)


def shards(field, beta, quartets, intersections):
    waves = jnp.asarray(host_waves())
    th, tl = (lax.axis_index(a).astype(jnp.int32)[None] for a in ("th", "tl"))
    weights = intersections.reshape(1, -1)
    along, across = (("th", "tl"), "mode")
    vmem = pl.BlockSpec(memory_space=pltpu.VMEM)
    smem = pl.BlockSpec(memory_space=pltpu.SMEM)
    limit = pltpu.CompilerParams(vmem_limit_bytes=16 * 1024 * 1024)

    def placed(kernel, state, *numbers):
        return pl.pallas_call(
            kernel,
            out_shape=rows_of(256),
            in_specs=[smem] * len(numbers) + [vmem],
            out_specs=vmem,
            compiler_params=limit,
        )(*numbers, state)

    def spectral(state):
        return pl.pallas_call(
            spectral_kernel,
            out_shape=rows_of(256),
            in_specs=[vmem] * 4,
            out_specs=vmem,
            compiler_params=limit,
        )(state, rotor, small, waves)

    square = jax.ShapeDtypeStruct((2, LANES, LANES), F32)
    small = pl.pallas_call(
        small_kernel,
        out_shape=square,
        in_specs=[smem],
        out_specs=vmem,
        compiler_params=limit,
        cost_estimate=pl.CostEstimate(flops=10**9, bytes_accessed=2 * TIME, transcendentals=0),
    )(th)
    rotor = pl.pallas_call(
        rotor_kernel,
        out_shape=square,
        in_specs=[smem] * 2 + [vmem] * 2,
        out_specs=vmem,
        compiler_params=limit,
        cost_estimate=pl.CostEstimate(flops=10**8, bytes_accessed=2 * TIME, transcendentals=0),
    )(th, tl, beta, small)
    state = pl.pallas_call(
        enter_kernel,
        out_shape=rows_of(256),
        in_specs=[vmem, vmem],
        out_specs=vmem,
        compiler_params=limit,
    )(field, rotor)
    state = exchange(state, along, 16)
    state = placed(first_radix_kernel, state, tl)
    state = exchange(state, "tl", 4)
    norms = []
    for step in range(STEPS):
        last = step == STEPS - 1
        state = spectral(state)
        state = exchange(state, along, 16)
        state = placed(back_kernel, state, th, tl)
        state = exchange(state, across, 32)
        out = pl.pallas_call(
            functools.partial(kerr_kernel, last),
            out_shape=rows_of(288) if last else (rows_of(256), rows_of(8)),
            in_specs=[vmem] * (3 + len(norms)),
            out_specs=vmem if last else (vmem, vmem),
            scratch_shapes=[pltpu.VMEM((256, LANES), F32)] if last else [],
            compiler_params=limit,
        )(state, quartets, weights, *norms)
        if last:
            state = exchange(out, across, 32)
            break
        state, norm = out
        norms.append(norm)
        state = exchange(state, across, 32)
        state = placed(ahead_kernel, state, th, tl)
        state = exchange(state, along, 16)
    state = pl.pallas_call(
        regroup_kernel,
        out_shape=rows_of(272),
        in_specs=[vmem],
        out_specs=vmem,
        compiler_params=limit,
    )(state)
    state = exchange(state, along, 16)
    return pl.pallas_call(
        leave_kernel,
        out_shape=(
            jax.ShapeDtypeStruct(field.shape, F32),
            jax.ShapeDtypeStruct((STEPS, field.shape[1]), F32),
        ),
        in_specs=[vmem],
        out_specs=(vmem, vmem),
        compiler_params=limit,
    )(state)


def solution(mesh):
    finer = Mesh(mesh.devices.reshape(-1, 4, 4), ("mode", "th", "tl"))
    times = ("th", "tl")
    return jax.shard_map(
        shards,
        mesh=finer,
        in_specs=(P(None, "mode", times), P(None, "mode"), P(), P()),
        out_specs=(P(None, "mode", times), P(None, "mode")),
        check_vma=False,
    )
```

```python
import functools
import math

import jax
import jax.numpy as jnp
import ml_dtypes
import numpy as np
from jax import lax
from jax.experimental import pallas as pl
from jax.experimental.pallas import tpu as pltpu
from jax.sharding import Mesh
from jax.sharding import PartitionSpec as P

STEPS = 2
LANES = 128
TIME = 65536
QUARTER = TIME // 4
TILE = 256
EPSILON = 1e-06
F32 = jnp.float32
BF16 = jnp.bfloat16


def two_parts(table):
    high = table.astype(ml_dtypes.bfloat16)
    low = (table - high.astype(np.float64)).astype(ml_dtypes.bfloat16)
    return np.stack([high, low])


@functools.cache
def host_waves():
    index = np.arange(LANES)
    wave = np.exp(-2j * math.pi / LANES * (index[:, None] * index[None, :] % LANES))
    ahead = np.block([[wave.real, -wave.imag], [wave.imag, wave.real]])
    back = np.block([[wave.real, wave.imag], [-wave.imag, wave.real]])

    def row_order(place):
        return np.array([ri * LANES + p for p, ri in place])

    tile_order = row_order(
        [(v * 16 + w, ri) for w in range(16) for ri in range(2) for v in range(8)]
    )
    tables = (ahead[:, tile_order], ahead.T, back.T, back[tile_order] / TIME)
    return np.stack([two_parts(table) for table in tables])


def split(array):
    high = array.astype(BF16)
    return (high, (array - high.astype(F32)).astype(BF16))


def dot(left, right):
    return jnp.dot(left, right, preferred_element_type=F32)


def from_left(waves_ref, which, array):
    high, low = split(array)
    return dot(waves_ref[which, 0], high) + (
        dot(waves_ref[which, 0], low) + dot(waves_ref[which, 1], high)
    )


def from_right(array, waves_ref, which):
    high, low = split(array)
    return dot(high, waves_ref[which, 0]) + (
        dot(low, waves_ref[which, 0]) + dot(high, waves_ref[which, 1])
    )


def small_cosine_and_sine(x):
    z = x * x
    sine = ((-1.9515295891e-4 * z + 8.3321608736e-3) * z - 1.6666654611e-1) * z * x + x
    cosine = (
        (2.443315711809948e-5 * z - 1.388731625493765e-3) * z + 4.166664568298827e-2
    ) * z * z - 0.5 * z + 1.0
    return (cosine, sine)


def in_quarter(turns, cosine, sine):
    quarter = turns & 3
    odd = (quarter & 1) == 1
    c = jnp.where(odd, sine, cosine)
    s = jnp.where(odd, cosine, sine)
    c = jnp.where((quarter == 1) | (quarter == 2), -c, c)
    s = jnp.where(quarter >= 2, -s, s)
    return (c, s)


def cosine_and_sine(angle):
    scaled = angle * (2.0 / math.pi)
    turns = (scaled + jnp.where(scaled >= 0.0, 0.5, -0.5)).astype(jnp.int32)
    count = turns.astype(F32)
    x = angle - count * 1.5703125
    x = x - count * 4.837512969970703125e-4
    x = x - count * 7.5497899548918822e-8
    return in_quarter(turns, *small_cosine_and_sine(x))


def twist(number):
    turns = (number + TIME // 8) >> 14
    rest = (number - (turns << 14)).astype(F32)
    return in_quarter(turns, *small_cosine_and_sine(rest * (2.0 * math.pi / TIME)))


def row_and_lane():
    return (lax.broadcasted_iota(jnp.int32, (8, LANES), axis) for axis in range(2))


def small_kernel(th_ref, small_ref):
    row, lane = (lax.broadcasted_iota(jnp.int32, (LANES, LANES), axis) for axis in range(2))
    small_ref[0], small_ref[1] = twist(4 * row * lane)


def rotor_kernel(th_ref, tl_ref, beta_ref, after_ref, rotor_ref):
    own = lax.broadcasted_iota(jnp.int32, beta_ref.shape, 1) == th_ref[0]
    beta = jnp.sum(jnp.where(own, beta_ref[...], 0.0), axis=1, keepdims=True)
    offset, slope, curve = (beta[k : k + 1, :] for k in range(3))
    row, lane = (lax.broadcasted_iota(jnp.int32, (LANES, LANES), axis) for axis in range(2))
    wave = 4 * (row + LANES * lane) + tl_ref[0]
    signed = jnp.where(wave < TIME // 2, wave, wave - TIME)
    frequency = signed.astype(F32) * (1.0 / (TIME / 2))
    angle = (
        math.pi * offset
        + 300.0 * slope * frequency
        + 3000.0 * curve * frequency * frequency
    )
    rotor_ref[0], rotor_ref[1] = cosine_and_sine(angle)


def enter_kernel(field_ref, after_ref, out_ref):
    for ri in range(2):
        for tile in range(32):
            zb, rest = (tile // 4 % 4, tile // 16 * 4 + tile % 4)
            out_ref[pl.ds(zb * 16 + ri * 8 + rest, 4, stride=64), :] = field_ref[
                ri, :, tile * LANES : (tile + 1) * LANES
            ]


def radix_ahead(x):
    (r0, i0), (r1, i1), (r2, i2), (r3, i3) = x
    sr, si, dr, di = r0 + r2, i0 + i2, r0 - r2, i0 - i2
    tr, ti, ur, ui = r1 + r3, i1 + i3, r1 - r3, i1 - i3
    return [(sr + tr, si + ti), (dr + ui, di - ur), (sr - tr, si - ti), (dr - ui, di + ur)]


def radix_back(x):
    out = radix_ahead(x)
    return [out[0], out[3], out[2], out[1]]


def turned_back(pair, c, s):
    re, im = pair
    return (re * c + im * s, im * c - re * s)


def turned(pair, c, s):
    return turned_back(pair, c, -s)


def first_radix_kernel(zb_ref, x_ref, out_ref):
    row, lane = row_and_lane()
    place = (row // 4) * 2048 + (row % 4) * LANES + lane + zb_ref[0] * 512
    for v2 in range(4):
        at = [a * 64 + v2 * 16 for a in range(4)]
        y = radix_ahead([(x_ref[b : b + 8, :], x_ref[b + 8 : b + 16, :]) for b in at])
        for f in range(4):
            pair = turned_back(y[f], *twist(f * (place + v2 * 4096))) if f else y[f]
            for ri in range(2):
                for v0 in range(2):
                    first = f * 64 + ri * 8 + v2 * 2 + v0
                    out_ref[pl.ds(first, 4, stride=16), :] = pair[ri][v0 * 4 : v0 * 4 + 4]


def middle_twists(th_ref, tl_ref):
    row, lane = row_and_lane()
    place = row * 2048 + lane + (th_ref[0] * 4 + tl_ref[0]) * LANES
    return [None] + [twist(f * place) for f in range(1, 4)]


def ahead_kernel(th_ref, tl_ref, x_ref, out_ref):
    twists = middle_twists(th_ref, tl_ref)
    for low in range(4):
        y = radix_ahead(
            [
                tuple(x_ref[pl.ds(a * 64 + low * 2 + ri, 8, stride=8), :] for ri in range(2))
                for a in range(4)
            ]
        )
        for f in range(4):
            re, im = turned_back(y[f], *twists[f]) if f else y[f]
            at = low * 64 + f * 16
            out_ref[at : at + 8, :] = re
            out_ref[at + 8 : at + 16, :] = im


def back_kernel(th_ref, tl_ref, x_ref, out_ref):
    twists = middle_twists(th_ref, tl_ref)
    for low in range(4):
        y = []
        for f in range(4):
            at = low * 64 + f * 16
            pair = (x_ref[at : at + 8, :], x_ref[at + 8 : at + 16, :])
            y.append(turned(pair, *twists[f]) if f else pair)
        for a, pair in enumerate(radix_back(y)):
            for ri in range(2):
                out_ref[pl.ds(a * 64 + low * 2 + ri, 8, stride=8), :] = pair[ri]


def spectral_kernel(x_ref, rotor_ref, small_ref, waves_ref, out_ref):
    rotor = (rotor_ref[0], rotor_ref[1])
    small = (small_ref[0], small_ref[1])
    y = from_left(waves_ref, 0, x_ref[...])
    re, im = turned_back((y[:LANES], y[LANES:]), *small)
    y = from_right(jnp.concatenate([re, im], axis=1), waves_ref, 1)
    re, im = turned((y[:, :LANES], y[:, LANES:]), *rotor)
    y = from_right(jnp.concatenate([re, im], axis=1), waves_ref, 2)
    re, im = turned((y[:, :LANES], y[:, LANES:]), *small)
    out_ref[...] = from_left(waves_ref, 3, jnp.concatenate([re, im], axis=0))


def one_hots(quartets_ref, modes):
    row = lax.broadcasted_iota(jnp.int32, (modes, 1), 0)
    x, core, y, low = (row >> 5, (row >> 4) & 1, (row >> 2) & 3, row & 3)
    ids = ((y * 4 + x) * 2 + core) * 4 + low
    return [
        jnp.where(quartets_ref[k : k + 1, :] == ids, 1.0, 0.0).astype(BF16) for k in range(4)
    ]


def kerr_term(fields, hot, weights_ref):
    size = fields.shape[0] // 2
    parts = jnp.concatenate(split(fields), axis=1)
    total = None
    for start in range(0, weights_ref.shape[1], TILE):
        here = slice(start, start + TILE)
        (lr, li), (mr, mi), (nr, ni) = (
            (y[:size], y[size:])
            for y in (dot(parts, jnp.concatenate([hot[k][:, here]] * 2, axis=0)) for k in (1, 2, 3))
        )
        weight = weights_ref[:, here]
        pr, pi = (lr * mr - li * mi, lr * mi + li * mr)
        pr, pi = (pr * weight, pi * weight)
        terms = jnp.concatenate([pr * ni - pi * nr, pr * nr + pi * ni], axis=0)
        terms = jnp.concatenate(split(terms), axis=1)
        added = lax.dot_general(
            terms,
            jnp.concatenate([hot[0][:, here]] * 2, axis=1),
            (((1,), (1,)), ((), ())),
            preferred_element_type=F32,
        )
        total = added if total is None else total + added
    return total


def kerr_kernel(last, x_ref, quartets_ref, weights_ref, *refs):
    modes = x_ref.shape[0] // 2
    linear = jnp.concatenate(
        [x_ref[pl.ds(ri, modes, stride=2), :].T for ri in range(2)], axis=0
    )
    hot = one_hots(quartets_ref, modes)
    first = kerr_term(linear, hot, weights_ref)
    second = kerr_term(linear + first, hot, weights_ref)
    updated = linear + 0.5 * (first + second)
    estimate = 0.5 * (second - first)
    sums = [jnp.sum(y * y, axis=0, keepdims=True) for y in (estimate, updated)]
    if not last:
        out_ref, sums_ref = refs
        for ri in range(2):
            out_ref[pl.ds(ri, modes, stride=2), :] = updated[ri * LANES : (ri + 1) * LANES].T
        sums_ref[0:1, :] = sums[0]
        sums_ref[1:2, :] = sums[1]
        return
    before_ref, out_ref, held_ref = refs
    for ri in range(2):
        held_ref[pl.ds(ri, modes, stride=2), :] = updated[ri * LANES : (ri + 1) * LANES].T
    norms = [before_ref[0:1, :], before_ref[1:2, :], *sums]
    shape = (modes // 4, modes)
    own = lax.broadcasted_iota(jnp.int32, shape, 1) // 4 == lax.broadcasted_iota(jnp.int32, shape, 0)
    picked = jnp.concatenate([jnp.where(own, norm, 0.0) for norm in norms], axis=1)
    shape = (4 * modes, LANES)
    source = lax.broadcasted_iota(jnp.int32, shape, 0)
    target = source // modes * 4 + source % 4
    moves = jnp.where(lax.broadcasted_iota(jnp.int32, shape, 1) == target, 1.0, 0.0).astype(BF16)
    high, low = split(picked)
    rows = dot(high, moves) + dot(low, moves)
    for group in range(modes // 4):
        out_ref[group * 9 : group * 9 + 8, :] = held_ref[group * 8 : group * 8 + 8, :]
        out_ref[group * 9 + 8 : group * 9 + 9, :] = rows[group : group + 1, :]


def regroup_kernel(x_ref, out_ref):
    norms = x_ref[8:9, :]
    for source in range(1, 32):
        norms = norms + x_ref[source * 9 + 8 : source * 9 + 9, :]
    for target in range(16):
        for half in range(2):
            source = target * 2 + half
            at = target * 17 + half * 8
            out_ref[at : at + 8, :] = x_ref[source * 9 : source * 9 + 8, :]
        out_ref[target * 17 + 16 : target * 17 + 17, :] = norms


def leave_kernel(x_ref, field_ref, errors_ref):
    norms = x_ref[16:17, :]
    for source in range(1, 16):
        norms = norms + x_ref[source * 17 + 16 : source * 17 + 17, :]
    size = pltpu.roll(norms, LANES - 4, 1)
    ratio = jnp.sqrt(norms / (size + EPSILON))
    errors_ref[0:1, :] = ratio[:, 0:4]
    errors_ref[1:2, :] = ratio[:, 8:12]
    for source in range(16):
        for half in range(2):
            tile = half * 16 + source
            for ri in range(2):
                field_ref[ri, :, tile * LANES : (tile + 1) * LANES] = x_ref[
                    pl.ds(source * 17 + half * 8 + ri, 4, stride=2), :
                ]


def rows_of(count):
    return jax.ShapeDtypeStruct((count, LANES), F32)


def exchange(array, axes, peers):
    rows = array.shape[0] // peers
    tile = 8 if rows % 8 == 0 else 1
    tiles = array.reshape(peers, rows // tile, tile, LANES)
    return lax.all_to_all(tiles, axes, 0, 0, tiled=True).reshape(array.shape)


def shards(field, beta, quartets, intersections):
    waves = jnp.asarray(host_waves())
    th, tl = (lax.axis_index(a).astype(jnp.int32)[None] for a in ("th", "tl"))
    weights = intersections.reshape(1, -1)
    along, across = (("th", "tl"), ("x", "core", "y"))
    vmem = pl.BlockSpec(memory_space=pltpu.VMEM)
    smem = pl.BlockSpec(memory_space=pltpu.SMEM)
    limit = pltpu.CompilerParams(vmem_limit_bytes=16 * 1024 * 1024)

    def placed(kernel, state, *numbers):
        return pl.pallas_call(
            kernel,
            out_shape=rows_of(256),
            in_specs=[smem] * len(numbers) + [vmem],
            out_specs=vmem,
            compiler_params=limit,
        )(*numbers, state)

    def spectral(state):
        return pl.pallas_call(
            spectral_kernel,
            out_shape=rows_of(256),
            in_specs=[vmem] * 4,
            out_specs=vmem,
            compiler_params=limit,
        )(state, rotor, small, waves)

    square = jax.ShapeDtypeStruct((2, LANES, LANES), F32)
    small = pl.pallas_call(
        small_kernel,
        out_shape=square,
        in_specs=[smem],
        out_specs=vmem,
        compiler_params=limit,
        cost_estimate=pl.CostEstimate(flops=10**9, bytes_accessed=2 * TIME, transcendentals=0),
    )(th)
    rotor = pl.pallas_call(
        rotor_kernel,
        out_shape=square,
        in_specs=[smem] * 2 + [vmem] * 2,
        out_specs=vmem,
        compiler_params=limit,
        cost_estimate=pl.CostEstimate(flops=10**8, bytes_accessed=2 * TIME, transcendentals=0),
    )(th, tl, beta, small)
    state = pl.pallas_call(
        enter_kernel,
        out_shape=rows_of(256),
        in_specs=[vmem, vmem],
        out_specs=vmem,
        compiler_params=limit,
    )(field, rotor)
    state = exchange(state, along, 16)
    state = placed(first_radix_kernel, state, tl)
    state = exchange(state, "tl", 4)
    norms = []
    for step in range(STEPS):
        last = step == STEPS - 1
        state = spectral(state)
        state = exchange(state, along, 16)
        state = placed(back_kernel, state, th, tl)
        state = exchange(state, across, 32)
        out = pl.pallas_call(
            functools.partial(kerr_kernel, last),
            out_shape=rows_of(288) if last else (rows_of(256), rows_of(8)),
            in_specs=[vmem] * (3 + len(norms)),
            out_specs=vmem if last else (vmem, vmem),
            scratch_shapes=[pltpu.VMEM((256, LANES), F32)] if last else [],
            compiler_params=limit,
        )(state, quartets, weights, *norms)
        if last:
            state = exchange(out, across, 32)
            break
        state, norm = out
        norms.append(norm)
        state = exchange(state, across, 32)
        state = placed(ahead_kernel, state, th, tl)
        state = exchange(state, along, 16)
    state = pl.pallas_call(
        regroup_kernel,
        out_shape=rows_of(272),
        in_specs=[vmem],
        out_specs=vmem,
        compiler_params=limit,
    )(state)
    state = exchange(state, along, 16)
    return pl.pallas_call(
        leave_kernel,
        out_shape=(
            jax.ShapeDtypeStruct(field.shape, F32),
            jax.ShapeDtypeStruct((STEPS, field.shape[1]), F32),
        ),
        in_specs=[vmem],
        out_specs=(vmem, vmem),
        compiler_params=limit,
    )(state)


def solution(mesh):
    finer = Mesh(mesh.devices.reshape(4, 4, 2, 4, 4), ("y", "x", "core", "th", "tl"))
    modes, times = (("y", "x", "core"), ("th", "tl"))
    return jax.shard_map(
        shards,
        mesh=finer,
        in_specs=(P(None, modes, times), P(None, modes), P(), P()),
        out_specs=(P(None, modes, times), P(None, modes)),
        check_vma=False,
    )
```

```python
import functools
import math

import jax
import jax.numpy as jnp
import ml_dtypes
import numpy as np
from jax import lax
from jax.experimental import pallas as pl
from jax.experimental.pallas import tpu as pltpu
from jax.sharding import Mesh
from jax.sharding import PartitionSpec as P

STEPS = 2
LANES = 128
BACKWARD = (0, 2, 1, 3)
TIME = 65536
QUARTER = TIME // 4
TILE = 256
EPSILON = 1e-06
F32 = jnp.float32
BF16 = jnp.bfloat16


def two_parts(table):
    high = table.astype(ml_dtypes.bfloat16)
    low = (table - high.astype(np.float64)).astype(ml_dtypes.bfloat16)
    return np.stack([high, low])


@functools.cache
def host_waves():
    index = np.arange(LANES)
    wave = np.exp(-2j * math.pi / LANES * (index[:, None] * index[None, :] % LANES))
    ahead = np.block([[wave.real, -wave.imag], [wave.imag, wave.real]])
    back = np.block([[wave.real, wave.imag], [-wave.imag, wave.real]])

    def row_order(place):
        return np.array([ri * LANES + p for p, ri in place])

    tile_order = row_order(
        [(v * 16 + w, ri) for w in range(16) for ri in range(2) for v in range(8)]
    )
    tables = (ahead[:, tile_order], ahead.T, back.T, back[tile_order] / TIME)
    return np.stack([two_parts(table) for table in tables])


def split(array):
    high = array.astype(BF16)
    return (high, (array - high.astype(F32)).astype(BF16))


def dot(left, right):
    return jnp.dot(left, right, preferred_element_type=F32)


def from_left(waves_ref, which, array):
    high, low = split(array)
    return dot(waves_ref[which, 0], high) + (
        dot(waves_ref[which, 0], low) + dot(waves_ref[which, 1], high)
    )


def from_right(array, waves_ref, which):
    high, low = split(array)
    return dot(high, waves_ref[which, 0]) + (
        dot(low, waves_ref[which, 0]) + dot(high, waves_ref[which, 1])
    )


def small_cosine_and_sine(x):
    z = x * x
    sine = ((-1.9515295891e-4 * z + 8.3321608736e-3) * z - 1.6666654611e-1) * z * x + x
    cosine = (
        (2.443315711809948e-5 * z - 1.388731625493765e-3) * z + 4.166664568298827e-2
    ) * z * z - 0.5 * z + 1.0
    return (cosine, sine)


def in_quarter(turns, cosine, sine):
    quarter = turns & 3
    odd = (quarter & 1) == 1
    c = jnp.where(odd, sine, cosine)
    s = jnp.where(odd, cosine, sine)
    c = jnp.where((quarter == 1) | (quarter == 2), -c, c)
    s = jnp.where(quarter >= 2, -s, s)
    return (c, s)


def cosine_and_sine(angle):
    scaled = angle * (2.0 / math.pi)
    turns = (scaled + jnp.where(scaled >= 0.0, 0.5, -0.5)).astype(jnp.int32)
    count = turns.astype(F32)
    x = angle - count * 1.5703125
    x = x - count * 4.837512969970703125e-4
    x = x - count * 7.5497899548918822e-8
    return in_quarter(turns, *small_cosine_and_sine(x))


def twist(number):
    turns = (number + TIME // 8) >> 14
    rest = (number - (turns << 14)).astype(F32)
    return in_quarter(turns, *small_cosine_and_sine(rest * (2.0 * math.pi / TIME)))


def row_and_lane():
    return (lax.broadcasted_iota(jnp.int32, (8, LANES), axis) for axis in range(2))


def small_kernel(th_ref, small_ref):
    row, lane = (lax.broadcasted_iota(jnp.int32, (LANES, LANES), axis) for axis in range(2))
    small_ref[0], small_ref[1] = twist(4 * row * lane)


def rotor_kernel(th_ref, tl_ref, beta_ref, after_ref, rotor_ref):
    own = lax.broadcasted_iota(jnp.int32, beta_ref.shape, 1) == th_ref[0]
    beta = jnp.sum(jnp.where(own, beta_ref[...], 0.0), axis=1, keepdims=True)
    offset, slope, curve = (beta[k : k + 1, :] for k in range(3))
    row, lane = (lax.broadcasted_iota(jnp.int32, (LANES, LANES), axis) for axis in range(2))
    wave = 4 * (row + LANES * lane) + tl_ref[0]
    signed = jnp.where(wave < TIME // 2, wave, wave - TIME)
    frequency = signed.astype(F32) * (1.0 / (TIME / 2))
    angle = (
        math.pi * offset
        + 300.0 * slope * frequency
        + 3000.0 * curve * frequency * frequency
    )
    rotor_ref[0], rotor_ref[1] = cosine_and_sine(angle)


def enter_kernel(field_ref, after_ref, out_ref):
    for ri in range(2):
        for tile in range(32):
            zb, rest = (tile // 4 % 4, tile // 16 * 4 + tile % 4)
            out_ref[pl.ds(zb * 16 + ri * 8 + rest, 4, stride=64), :] = field_ref[
                ri, :, tile * LANES : (tile + 1) * LANES
            ]


def radix_ahead(x):
    (r0, i0), (r1, i1), (r2, i2), (r3, i3) = x
    sr, si, dr, di = r0 + r2, i0 + i2, r0 - r2, i0 - i2
    tr, ti, ur, ui = r1 + r3, i1 + i3, r1 - r3, i1 - i3
    return [(sr + tr, si + ti), (dr + ui, di - ur), (sr - tr, si - ti), (dr - ui, di + ur)]


def radix_back(x):
    out = radix_ahead(x)
    return [out[0], out[3], out[2], out[1]]


def turned_back(pair, c, s):
    re, im = pair
    return (re * c + im * s, im * c - re * s)


def turned(pair, c, s):
    return turned_back(pair, c, -s)


def first_radix_kernel(zb_ref, x_ref, out_ref):
    row, lane = row_and_lane()
    place = (row // 4) * 2048 + (row % 4) * LANES + lane + zb_ref[0] * 512
    for v2 in range(4):
        at = [a * 64 + v2 * 16 for a in range(4)]
        y = radix_ahead([(x_ref[b : b + 8, :], x_ref[b + 8 : b + 16, :]) for b in at])
        for f in range(4):
            pair = turned_back(y[f], *twist(f * (place + v2 * 4096))) if f else y[f]
            for ri in range(2):
                for v0 in range(2):
                    first = BACKWARD[f] * 64 + ri * 8 + v2 * 2 + v0
                    out_ref[pl.ds(first, 4, stride=16), :] = pair[ri][v0 * 4 : v0 * 4 + 4]


def middle_twists(th_ref, tl_ref):
    row, lane = row_and_lane()
    place = row * 2048 + lane + (th_ref[0] * 4 + tl_ref[0]) * LANES
    return [None] + [twist(f * place) for f in range(1, 4)]


def ahead_kernel(th_ref, tl_ref, x_ref, out_ref):
    twists = middle_twists(th_ref, tl_ref)
    for low in range(4):
        y = radix_ahead(
            [
                tuple(x_ref[pl.ds(a * 64 + low * 2 + ri, 8, stride=8), :] for ri in range(2))
                for a in range(4)
            ]
        )
        for f in range(4):
            re, im = turned_back(y[f], *twists[f]) if f else y[f]
            at = low * 64 + f * 16
            out_ref[at : at + 8, :] = re
            out_ref[at + 8 : at + 16, :] = im


def back_kernel(th_ref, tl_ref, x_ref, out_ref):
    twists = middle_twists(th_ref, tl_ref)
    for low in range(4):
        y = []
        for f in range(4):
            at = low * 64 + f * 16
            pair = (x_ref[at : at + 8, :], x_ref[at + 8 : at + 16, :])
            y.append(turned(pair, *twists[f]) if f else pair)
        for a, pair in enumerate(radix_back(y)):
            for ri in range(2):
                out_ref[pl.ds(a * 64 + low * 2 + ri, 8, stride=8), :] = pair[ri]


def spectral_kernel(order, x_ref, rotor_ref, small_ref, waves_ref, out_ref):
    rotor = (rotor_ref[0], rotor_ref[1])
    small = (small_ref[0], small_ref[1])
    x = jnp.concatenate([x_ref[64 * k : 64 * k + 64, :] for k in order], axis=0)
    y = from_left(waves_ref, 0, x)
    re, im = turned_back((y[:LANES], y[LANES:]), *small)
    y = from_right(jnp.concatenate([re, im], axis=1), waves_ref, 1)
    re, im = turned((y[:, :LANES], y[:, LANES:]), *rotor)
    y = from_right(jnp.concatenate([re, im], axis=1), waves_ref, 2)
    re, im = turned((y[:, :LANES], y[:, LANES:]), *small)
    out_ref[...] = from_left(waves_ref, 3, jnp.concatenate([re, im], axis=0))


def one_hots(quartets_ref, modes):
    ids = lax.broadcasted_iota(jnp.int32, (modes, quartets_ref.shape[1]), 0)
    return [
        jnp.where(quartets_ref[k : k + 1, :] == ids, 1.0, 0.0).astype(BF16) for k in range(4)
    ]


def kerr_term(fields, hot, weights_ref):
    size = fields.shape[0] // 2
    parts = jnp.concatenate(split(fields), axis=1)
    total = None
    for start in range(0, weights_ref.shape[1], TILE):
        here = slice(start, start + TILE)
        (lr, li), (mr, mi), (nr, ni) = (
            (y[:size], y[size:])
            for y in (dot(parts, jnp.concatenate([hot[k][:, here]] * 2, axis=0)) for k in (1, 2, 3))
        )
        weight = weights_ref[:, here]
        pr, pi = (lr * mr - li * mi, lr * mi + li * mr)
        pr, pi = (pr * weight, pi * weight)
        terms = jnp.concatenate([pr * ni - pi * nr, pr * nr + pi * ni], axis=0)
        terms = jnp.concatenate(split(terms), axis=1)
        added = lax.dot_general(
            terms,
            jnp.concatenate([hot[0][:, here]] * 2, axis=1),
            (((1,), (1,)), ((), ())),
            preferred_element_type=F32,
        )
        total = added if total is None else total + added
    return total


def kerr_kernel(last, x_ref, quartets_ref, weights_ref, *refs):
    modes = x_ref.shape[0] // 2
    linear = jnp.concatenate(
        [x_ref[pl.ds(ri, modes, stride=2), :].T for ri in range(2)], axis=0
    )
    hot = one_hots(quartets_ref, modes)
    first = kerr_term(linear, hot, weights_ref)
    second = kerr_term(linear + first, hot, weights_ref)
    updated = linear + 0.5 * (first + second)
    estimate = 0.5 * (second - first)
    sums = [jnp.sum(y * y, axis=0, keepdims=True) for y in (estimate, updated)]
    if not last:
        out_ref, sums_ref = refs
        for ri in range(2):
            out_ref[pl.ds(ri, modes, stride=2), :] = updated[ri * LANES : (ri + 1) * LANES].T
        sums_ref[0:1, :] = sums[0]
        sums_ref[1:2, :] = sums[1]
        return
    before_ref, out_ref, held_ref = refs
    for ri in range(2):
        held_ref[pl.ds(ri, modes, stride=2), :] = updated[ri * LANES : (ri + 1) * LANES].T
    norms = [before_ref[0:1, :], before_ref[1:2, :], *sums]
    shape = (modes // 4, modes)
    own = lax.broadcasted_iota(jnp.int32, shape, 1) // 4 == lax.broadcasted_iota(jnp.int32, shape, 0)
    picked = jnp.concatenate([jnp.where(own, norm, 0.0) for norm in norms], axis=1)
    shape = (4 * modes, LANES)
    source = lax.broadcasted_iota(jnp.int32, shape, 0)
    target = source // modes * 4 + source % 4
    moves = jnp.where(lax.broadcasted_iota(jnp.int32, shape, 1) == target, 1.0, 0.0).astype(BF16)
    high, low = split(picked)
    rows = dot(high, moves) + dot(low, moves)
    for group in range(modes // 4):
        out_ref[group * 9 : group * 9 + 8, :] = held_ref[group * 8 : group * 8 + 8, :]
        out_ref[group * 9 + 8 : group * 9 + 9, :] = rows[group : group + 1, :]


def regroup_kernel(x_ref, out_ref):
    norms = x_ref[8:9, :]
    for source in range(1, 32):
        norms = norms + x_ref[source * 9 + 8 : source * 9 + 9, :]
    for target in range(16):
        for half in range(2):
            source = target * 2 + half
            at = target * 17 + half * 8
            out_ref[at : at + 8, :] = x_ref[source * 9 : source * 9 + 8, :]
        out_ref[target * 17 + 16 : target * 17 + 17, :] = norms


def leave_kernel(x_ref, field_ref, errors_ref):
    norms = x_ref[16:17, :]
    for source in range(1, 16):
        norms = norms + x_ref[source * 17 + 16 : source * 17 + 17, :]
    size = pltpu.roll(norms, LANES - 4, 1)
    ratio = jnp.sqrt(norms / (size + EPSILON))
    errors_ref[0:1, :] = ratio[:, 0:4]
    errors_ref[1:2, :] = ratio[:, 8:12]
    for source in range(16):
        for half in range(2):
            tile = half * 16 + source
            for ri in range(2):
                field_ref[ri, :, tile * LANES : (tile + 1) * LANES] = x_ref[
                    pl.ds(source * 17 + half * 8 + ri, 4, stride=2), :
                ]


def rows_of(count):
    return jax.ShapeDtypeStruct((count, LANES), F32)


def exchange(array, axes, peers):
    rows = array.shape[0] // peers
    tile = 8 if rows % 8 == 0 else 1
    tiles = array.reshape(peers, rows // tile, tile, LANES)
    return lax.all_to_all(tiles, axes, 0, 0, tiled=True).reshape(array.shape)


def shards(field, beta, quartets, intersections):
    waves = jnp.asarray(host_waves())
    th, tl = (lax.axis_index(a).astype(jnp.int32)[None] for a in ("th", ("t1", "t0")))
    weights = intersections.reshape(1, -1)
    along, across = (("th", "t1", "t0"), "mode")
    vmem = pl.BlockSpec(memory_space=pltpu.VMEM)
    smem = pl.BlockSpec(memory_space=pltpu.SMEM)
    limit = pltpu.CompilerParams(vmem_limit_bytes=16 * 1024 * 1024)

    def placed(kernel, state, *numbers):
        return pl.pallas_call(
            kernel,
            out_shape=rows_of(256),
            in_specs=[smem] * len(numbers) + [vmem],
            out_specs=vmem,
            compiler_params=limit,
        )(*numbers, state)

    def spectral(state, order):
        return pl.pallas_call(
            functools.partial(spectral_kernel, order),
            out_shape=rows_of(256),
            in_specs=[vmem] * 4,
            out_specs=vmem,
            compiler_params=limit,
        )(state, rotor, small, waves)

    square = jax.ShapeDtypeStruct((2, LANES, LANES), F32)
    small = pl.pallas_call(
        small_kernel,
        out_shape=square,
        in_specs=[smem],
        out_specs=vmem,
        compiler_params=limit,
        cost_estimate=pl.CostEstimate(flops=10**9, bytes_accessed=2 * TIME, transcendentals=0),
    )(th)
    rotor = pl.pallas_call(
        rotor_kernel,
        out_shape=square,
        in_specs=[smem] * 2 + [vmem] * 2,
        out_specs=vmem,
        compiler_params=limit,
        cost_estimate=pl.CostEstimate(flops=10**8, bytes_accessed=2 * TIME, transcendentals=0),
    )(th, tl, beta, small)
    state = pl.pallas_call(
        enter_kernel,
        out_shape=rows_of(256),
        in_specs=[vmem, vmem],
        out_specs=vmem,
        compiler_params=limit,
    )(field, rotor)
    state = exchange(state, along, 16)
    state = placed(first_radix_kernel, state, tl)
    state = exchange(state, ("t0", "t1"), 4)
    norms = []
    for step in range(STEPS):
        last = step == STEPS - 1
        state = spectral(state, range(4) if step else BACKWARD)
        state = exchange(state, along, 16)
        state = placed(back_kernel, state, th, tl)
        state = exchange(state, across, 32)
        out = pl.pallas_call(
            functools.partial(kerr_kernel, last),
            out_shape=rows_of(288) if last else (rows_of(256), rows_of(8)),
            in_specs=[vmem] * (3 + len(norms)),
            out_specs=vmem if last else (vmem, vmem),
            scratch_shapes=[pltpu.VMEM((256, LANES), F32)] if last else [],
            compiler_params=limit,
        )(state, quartets, weights, *norms)
        if last:
            state = exchange(out, across, 32)
            break
        state, norm = out
        norms.append(norm)
        state = exchange(state, across, 32)
        state = placed(ahead_kernel, state, th, tl)
        state = exchange(state, along, 16)
    state = pl.pallas_call(
        regroup_kernel,
        out_shape=rows_of(272),
        in_specs=[vmem],
        out_specs=vmem,
        compiler_params=limit,
    )(state)
    state = exchange(state, along, 16)
    return pl.pallas_call(
        leave_kernel,
        out_shape=(
            jax.ShapeDtypeStruct(field.shape, F32),
            jax.ShapeDtypeStruct((STEPS, field.shape[1]), F32),
        ),
        in_specs=[vmem],
        out_specs=(vmem, vmem),
        compiler_params=limit,
    )(state)


def solution(mesh):
    finer = Mesh(mesh.devices.reshape(-1, 4, 2, 2), ("mode", "th", "t1", "t0"))
    times = ("th", "t1", "t0")
    return jax.shard_map(
        shards,
        mesh=finer,
        in_specs=(P(None, "mode", times), P(None, "mode"), P(), P()),
        out_specs=(P(None, "mode", times), P(None, "mode")),
        check_vma=False,
    )
```

```python
import functools
import math

import jax
import jax.numpy as jnp
import ml_dtypes
import numpy as np
from jax import lax
from jax.experimental import pallas as pl
from jax.experimental.pallas import tpu as pltpu
from jax.sharding import Mesh
from jax.sharding import PartitionSpec as P

STEPS = 2
LANES = 128
BACKWARD = (0, 2, 1, 3)
TIME = 65536
QUARTER = TIME // 4
TILE = 256
EPSILON = 1e-06
F32 = jnp.float32
BF16 = jnp.bfloat16


def two_parts(table):
    high = table.astype(ml_dtypes.bfloat16)
    low = (table - high.astype(np.float64)).astype(ml_dtypes.bfloat16)
    return np.stack([high, low])


@functools.cache
def host_waves():
    index = np.arange(LANES)
    wave = np.exp(-2j * math.pi / LANES * (index[:, None] * index[None, :] % LANES))
    ahead = np.block([[wave.real, -wave.imag], [wave.imag, wave.real]])
    back = np.block([[wave.real, wave.imag], [-wave.imag, wave.real]])

    def row_order(place):
        return np.array([ri * LANES + p for p, ri in place])

    tile_order = row_order(
        [(v * 16 + w, ri) for w in range(16) for ri in range(2) for v in range(8)]
    )
    tables = (ahead[:, tile_order], ahead.T, back.T, back[tile_order] / TIME)
    return np.stack([two_parts(table) for table in tables])


def split(array):
    high = array.astype(BF16)
    return (high, (array - high.astype(F32)).astype(BF16))


def dot(left, right):
    return jnp.dot(left, right, preferred_element_type=F32)


def from_left(waves_ref, which, array):
    high, low = split(array)
    return dot(waves_ref[which, 0], high) + (
        dot(waves_ref[which, 0], low) + dot(waves_ref[which, 1], high)
    )


def from_right(array, waves_ref, which):
    high, low = split(array)
    return dot(high, waves_ref[which, 0]) + (
        dot(low, waves_ref[which, 0]) + dot(high, waves_ref[which, 1])
    )


def small_cosine_and_sine(x):
    z = x * x
    sine = ((-1.9515295891e-4 * z + 8.3321608736e-3) * z - 1.6666654611e-1) * z * x + x
    cosine = (
        (2.443315711809948e-5 * z - 1.388731625493765e-3) * z + 4.166664568298827e-2
    ) * z * z - 0.5 * z + 1.0
    return (cosine, sine)


def in_quarter(turns, cosine, sine):
    quarter = turns & 3
    odd = (quarter & 1) == 1
    c = jnp.where(odd, sine, cosine)
    s = jnp.where(odd, cosine, sine)
    c = jnp.where((quarter == 1) | (quarter == 2), -c, c)
    s = jnp.where(quarter >= 2, -s, s)
    return (c, s)


def cosine_and_sine(angle):
    scaled = angle * (2.0 / math.pi)
    turns = (scaled + jnp.where(scaled >= 0.0, 0.5, -0.5)).astype(jnp.int32)
    count = turns.astype(F32)
    x = angle - count * 1.5703125
    x = x - count * 4.837512969970703125e-4
    x = x - count * 7.5497899548918822e-8
    return in_quarter(turns, *small_cosine_and_sine(x))


def twist(number):
    turns = (number + TIME // 8) >> 14
    rest = (number - (turns << 14)).astype(F32)
    return in_quarter(turns, *small_cosine_and_sine(rest * (2.0 * math.pi / TIME)))


def row_and_lane():
    return (lax.broadcasted_iota(jnp.int32, (8, LANES), axis) for axis in range(2))


def small_kernel(th_ref, small_ref):
    row, lane = (lax.broadcasted_iota(jnp.int32, (LANES, LANES), axis) for axis in range(2))
    small_ref[0], small_ref[1] = twist(4 * row * lane)


def rotor_kernel(th_ref, tl_ref, beta_ref, after_ref, rotor_ref):
    own = lax.broadcasted_iota(jnp.int32, beta_ref.shape, 1) == th_ref[0]
    beta = jnp.sum(jnp.where(own, beta_ref[...], 0.0), axis=1, keepdims=True)
    offset, slope, curve = (beta[k : k + 1, :] for k in range(3))
    row, lane = (lax.broadcasted_iota(jnp.int32, (LANES, LANES), axis) for axis in range(2))
    wave = 4 * (row + LANES * lane) + tl_ref[0]
    signed = jnp.where(wave < TIME // 2, wave, wave - TIME)
    frequency = signed.astype(F32) * (1.0 / (TIME / 2))
    angle = (
        math.pi * offset
        + 300.0 * slope * frequency
        + 3000.0 * curve * frequency * frequency
    )
    rotor_ref[0], rotor_ref[1] = cosine_and_sine(angle)


def enter_kernel(field_ref, after_ref, out_ref):
    for ri in range(2):
        for tile in range(32):
            zb, rest = (tile // 4 % 4, tile // 16 * 4 + tile % 4)
            at = BACKWARD[zb] * 16 + ri * 8 + rest
            out_ref[pl.ds(at, 4, stride=64), :] = field_ref[
                ri, :, tile * LANES : (tile + 1) * LANES
            ]


def radix_ahead(x):
    (r0, i0), (r1, i1), (r2, i2), (r3, i3) = x
    sr, si, dr, di = r0 + r2, i0 + i2, r0 - r2, i0 - i2
    tr, ti, ur, ui = r1 + r3, i1 + i3, r1 - r3, i1 - i3
    return [(sr + tr, si + ti), (dr + ui, di - ur), (sr - tr, si - ti), (dr - ui, di + ur)]


def radix_back(x):
    out = radix_ahead(x)
    return [out[0], out[3], out[2], out[1]]


def turned_back(pair, c, s):
    re, im = pair
    return (re * c + im * s, im * c - re * s)


def turned(pair, c, s):
    return turned_back(pair, c, -s)


def first_radix_kernel(zb_ref, x_ref, out_ref):
    row, lane = row_and_lane()
    place = (row // 4) * 2048 + (row % 4) * LANES + lane + zb_ref[0] * 512
    for v2 in range(4):
        at = [a * 64 + BACKWARD[v2] * 16 for a in range(4)]
        y = radix_ahead([(x_ref[b : b + 8, :], x_ref[b + 8 : b + 16, :]) for b in at])
        for f in range(4):
            pair = turned_back(y[f], *twist(f * (place + v2 * 4096))) if f else y[f]
            for ri in range(2):
                for v0 in range(2):
                    first = BACKWARD[f] * 64 + ri * 8 + v2 * 2 + v0
                    out_ref[pl.ds(first, 4, stride=16), :] = pair[ri][v0 * 4 : v0 * 4 + 4]


def middle_twists(th_ref, tl_ref):
    row, lane = row_and_lane()
    place = row * 2048 + lane + (th_ref[0] * 4 + tl_ref[0]) * LANES
    return [None] + [twist(f * place) for f in range(1, 4)]


def ahead_kernel(th_ref, tl_ref, x_ref, out_ref):
    twists = middle_twists(th_ref, tl_ref)
    for low in range(4):
        y = radix_ahead(
            [
                tuple(x_ref[pl.ds(a * 64 + low * 2 + ri, 8, stride=8), :] for ri in range(2))
                for a in range(4)
            ]
        )
        for f in range(4):
            re, im = turned_back(y[f], *twists[f]) if f else y[f]
            at = low * 64 + f * 16
            out_ref[at : at + 8, :] = re
            out_ref[at + 8 : at + 16, :] = im


def back_kernel(th_ref, tl_ref, x_ref, out_ref):
    twists = middle_twists(th_ref, tl_ref)
    for low in range(4):
        y = []
        for f in range(4):
            at = low * 64 + f * 16
            pair = (x_ref[at : at + 8, :], x_ref[at + 8 : at + 16, :])
            y.append(turned(pair, *twists[f]) if f else pair)
        for a, pair in enumerate(radix_back(y)):
            for ri in range(2):
                out_ref[pl.ds(a * 64 + low * 2 + ri, 8, stride=8), :] = pair[ri]


def spectral_kernel(order, x_ref, rotor_ref, small_ref, waves_ref, out_ref):
    rotor = (rotor_ref[0], rotor_ref[1])
    small = (small_ref[0], small_ref[1])
    x = jnp.concatenate([x_ref[64 * k : 64 * k + 64, :] for k in order], axis=0)
    y = from_left(waves_ref, 0, x)
    re, im = turned_back((y[:LANES], y[LANES:]), *small)
    y = from_right(jnp.concatenate([re, im], axis=1), waves_ref, 1)
    re, im = turned((y[:, :LANES], y[:, LANES:]), *rotor)
    y = from_right(jnp.concatenate([re, im], axis=1), waves_ref, 2)
    re, im = turned((y[:, :LANES], y[:, LANES:]), *small)
    out_ref[...] = from_left(waves_ref, 3, jnp.concatenate([re, im], axis=0))


def one_hots(quartets_ref, modes):
    ids = lax.broadcasted_iota(jnp.int32, (modes, quartets_ref.shape[1]), 0)
    return [
        jnp.where(quartets_ref[k : k + 1, :] == ids, 1.0, 0.0).astype(BF16) for k in range(4)
    ]


def kerr_term(fields, hot, weights_ref):
    size = fields.shape[0] // 2
    parts = jnp.concatenate(split(fields), axis=1)
    total = None
    for start in range(0, weights_ref.shape[1], TILE):
        here = slice(start, start + TILE)
        (lr, li), (mr, mi), (nr, ni) = (
            (y[:size], y[size:])
            for y in (dot(parts, jnp.concatenate([hot[k][:, here]] * 2, axis=0)) for k in (1, 2, 3))
        )
        weight = weights_ref[:, here]
        pr, pi = (lr * mr - li * mi, lr * mi + li * mr)
        pr, pi = (pr * weight, pi * weight)
        terms = jnp.concatenate([pr * ni - pi * nr, pr * nr + pi * ni], axis=0)
        terms = jnp.concatenate(split(terms), axis=1)
        added = lax.dot_general(
            terms,
            jnp.concatenate([hot[0][:, here]] * 2, axis=1),
            (((1,), (1,)), ((), ())),
            preferred_element_type=F32,
        )
        total = added if total is None else total + added
    return total


def kerr_kernel(last, x_ref, quartets_ref, weights_ref, *refs):
    modes = x_ref.shape[0] // 2
    linear = jnp.concatenate(
        [x_ref[pl.ds(ri, modes, stride=2), :].T for ri in range(2)], axis=0
    )
    hot = one_hots(quartets_ref, modes)
    first = kerr_term(linear, hot, weights_ref)
    second = kerr_term(linear + first, hot, weights_ref)
    updated = linear + 0.5 * (first + second)
    estimate = 0.5 * (second - first)
    sums = [jnp.sum(y * y, axis=0, keepdims=True) for y in (estimate, updated)]
    if not last:
        out_ref, sums_ref = refs
        for ri in range(2):
            out_ref[pl.ds(ri, modes, stride=2), :] = updated[ri * LANES : (ri + 1) * LANES].T
        sums_ref[0:1, :] = sums[0]
        sums_ref[1:2, :] = sums[1]
        return
    before_ref, out_ref, held_ref = refs
    for ri in range(2):
        held_ref[pl.ds(ri, modes, stride=2), :] = updated[ri * LANES : (ri + 1) * LANES].T
    norms = [before_ref[0:1, :], before_ref[1:2, :], *sums]
    shape = (modes // 4, modes)
    own = lax.broadcasted_iota(jnp.int32, shape, 1) // 4 == lax.broadcasted_iota(jnp.int32, shape, 0)
    picked = jnp.concatenate([jnp.where(own, norm, 0.0) for norm in norms], axis=1)
    shape = (4 * modes, LANES)
    source = lax.broadcasted_iota(jnp.int32, shape, 0)
    target = source // modes * 4 + source % 4
    moves = jnp.where(lax.broadcasted_iota(jnp.int32, shape, 1) == target, 1.0, 0.0).astype(BF16)
    high, low = split(picked)
    rows = dot(high, moves) + dot(low, moves)
    for group in range(modes // 4):
        out_ref[group * 9 : group * 9 + 8, :] = held_ref[group * 8 : group * 8 + 8, :]
        out_ref[group * 9 + 8 : group * 9 + 9, :] = rows[group : group + 1, :]


def regroup_kernel(x_ref, out_ref):
    norms = x_ref[8:9, :]
    for source in range(1, 32):
        norms = norms + x_ref[source * 9 + 8 : source * 9 + 9, :]
    for target in range(16):
        place = target // 4 * 4 + BACKWARD[target % 4]
        for half in range(2):
            source = target * 2 + half
            at = place * 17 + half * 8
            out_ref[at : at + 8, :] = x_ref[source * 9 : source * 9 + 8, :]
        out_ref[place * 17 + 16 : place * 17 + 17, :] = norms


def leave_kernel(x_ref, field_ref, errors_ref):
    norms = x_ref[16:17, :]
    for source in range(1, 16):
        norms = norms + x_ref[source * 17 + 16 : source * 17 + 17, :]
    size = pltpu.roll(norms, LANES - 4, 1)
    ratio = jnp.sqrt(norms / (size + EPSILON))
    errors_ref[0:1, :] = ratio[:, 0:4]
    errors_ref[1:2, :] = ratio[:, 8:12]
    for source in range(16):
        for half in range(2):
            tile = half * 16 + source // 4 * 4 + BACKWARD[source % 4]
            for ri in range(2):
                field_ref[ri, :, tile * LANES : (tile + 1) * LANES] = x_ref[
                    pl.ds(source * 17 + half * 8 + ri, 4, stride=2), :
                ]


def rows_of(count):
    return jax.ShapeDtypeStruct((count, LANES), F32)


def exchange(array, axes, peers):
    rows = array.shape[0] // peers
    tile = 8 if rows % 8 == 0 else 1
    tiles = array.reshape(peers, rows // tile, tile, LANES)
    return lax.all_to_all(tiles, axes, 0, 0, tiled=True).reshape(array.shape)


def shards(field, beta, quartets, intersections):
    waves = jnp.asarray(host_waves())
    th, tl = (lax.axis_index(a).astype(jnp.int32)[None] for a in ("th", ("t1", "t0")))
    weights = intersections.reshape(1, -1)
    along, across = (("th", "t1", "t0"), "mode")
    vmem = pl.BlockSpec(memory_space=pltpu.VMEM)
    smem = pl.BlockSpec(memory_space=pltpu.SMEM)
    limit = pltpu.CompilerParams(vmem_limit_bytes=16 * 1024 * 1024)

    def placed(kernel, state, *numbers):
        return pl.pallas_call(
            kernel,
            out_shape=rows_of(256),
            in_specs=[smem] * len(numbers) + [vmem],
            out_specs=vmem,
            compiler_params=limit,
        )(*numbers, state)

    def spectral(state, order):
        return pl.pallas_call(
            functools.partial(spectral_kernel, order),
            out_shape=rows_of(256),
            in_specs=[vmem] * 4,
            out_specs=vmem,
            compiler_params=limit,
        )(state, rotor, small, waves)

    square = jax.ShapeDtypeStruct((2, LANES, LANES), F32)
    small = pl.pallas_call(
        small_kernel,
        out_shape=square,
        in_specs=[smem],
        out_specs=vmem,
        compiler_params=limit,
        cost_estimate=pl.CostEstimate(flops=10**9, bytes_accessed=2 * TIME, transcendentals=0),
    )(th)
    rotor = pl.pallas_call(
        rotor_kernel,
        out_shape=square,
        in_specs=[smem] * 2 + [vmem] * 2,
        out_specs=vmem,
        compiler_params=limit,
        cost_estimate=pl.CostEstimate(flops=10**8, bytes_accessed=2 * TIME, transcendentals=0),
    )(th, tl, beta, small)
    state = pl.pallas_call(
        enter_kernel,
        out_shape=rows_of(256),
        in_specs=[vmem, vmem],
        out_specs=vmem,
        compiler_params=limit,
    )(field, rotor)
    state = exchange(state, ("th", "t0", "t1"), 16)
    state = placed(first_radix_kernel, state, tl)
    state = exchange(state, ("t0", "t1"), 4)
    norms = []
    for step in range(STEPS):
        last = step == STEPS - 1
        state = spectral(state, range(4) if step else BACKWARD)
        state = exchange(state, along, 16)
        state = placed(back_kernel, state, th, tl)
        state = exchange(state, across, 32)
        out = pl.pallas_call(
            functools.partial(kerr_kernel, last),
            out_shape=rows_of(288) if last else (rows_of(256), rows_of(8)),
            in_specs=[vmem] * (3 + len(norms)),
            out_specs=vmem if last else (vmem, vmem),
            scratch_shapes=[pltpu.VMEM((256, LANES), F32)] if last else [],
            compiler_params=limit,
        )(state, quartets, weights, *norms)
        if last:
            state = exchange(out, across, 32)
            break
        state, norm = out
        norms.append(norm)
        state = exchange(state, across, 32)
        state = placed(ahead_kernel, state, th, tl)
        state = exchange(state, along, 16)
    state = pl.pallas_call(
        regroup_kernel,
        out_shape=rows_of(272),
        in_specs=[vmem],
        out_specs=vmem,
        compiler_params=limit,
    )(state)
    state = exchange(state, ("th", "t0", "t1"), 16)
    return pl.pallas_call(
        leave_kernel,
        out_shape=(
            jax.ShapeDtypeStruct(field.shape, F32),
            jax.ShapeDtypeStruct((STEPS, field.shape[1]), F32),
        ),
        in_specs=[vmem],
        out_specs=(vmem, vmem),
        compiler_params=limit,
    )(state)


def solution(mesh):
    finer = Mesh(mesh.devices.reshape(-1, 4, 2, 2), ("mode", "th", "t1", "t0"))
    times = ("th", "t1", "t0")
    return jax.shard_map(
        shards,
        mesh=finer,
        in_specs=(P(None, "mode", times), P(None, "mode"), P(), P()),
        out_specs=(P(None, "mode", times), P(None, "mode")),
        check_vma=False,
    )
```

```python
import functools
import math

import jax
import jax.numpy as jnp
import ml_dtypes
import numpy as np
from jax import lax
from jax.experimental import pallas as pl
from jax.experimental.pallas import tpu as pltpu
from jax.sharding import Mesh
from jax.sharding import PartitionSpec as P

STEPS = 2
LANES = 128
BACKWARD = (0, 2, 1, 3)
TIME = 65536
QUARTER = TIME // 4
TILE = 256
EPSILON = 1e-06
F32 = jnp.float32
BF16 = jnp.bfloat16


def two_parts(table):
    high = table.astype(ml_dtypes.bfloat16)
    low = (table - high.astype(np.float64)).astype(ml_dtypes.bfloat16)
    return np.stack([high, low])


@functools.cache
def host_waves():
    index = np.arange(LANES)
    wave = np.exp(-2j * math.pi / LANES * (index[:, None] * index[None, :] % LANES))
    ahead = np.block([[wave.real, -wave.imag], [wave.imag, wave.real]])
    back = np.block([[wave.real, wave.imag], [-wave.imag, wave.real]])

    def row_order(place):
        return np.array([ri * LANES + p for p, ri in place])

    tile_order = row_order(
        [(v * 16 + w, ri) for w in range(16) for ri in range(2) for v in range(8)]
    )
    tables = (ahead[:, tile_order], ahead.T, back.T, back[tile_order] / TIME)
    return np.stack([two_parts(table) for table in tables])


def split(array):
    high = array.astype(BF16)
    return (high, (array - high.astype(F32)).astype(BF16))


def dot(left, right):
    return jnp.dot(left, right, preferred_element_type=F32)


def from_left(waves_ref, which, array):
    high, low = split(array)
    return dot(waves_ref[which, 0], high) + (
        dot(waves_ref[which, 0], low) + dot(waves_ref[which, 1], high)
    )


def from_right(array, waves_ref, which):
    high, low = split(array)
    return dot(high, waves_ref[which, 0]) + (
        dot(low, waves_ref[which, 0]) + dot(high, waves_ref[which, 1])
    )


def small_cosine_and_sine(x):
    z = x * x
    sine = ((-1.9515295891e-4 * z + 8.3321608736e-3) * z - 1.6666654611e-1) * z * x + x
    cosine = (
        (2.443315711809948e-5 * z - 1.388731625493765e-3) * z + 4.166664568298827e-2
    ) * z * z - 0.5 * z + 1.0
    return (cosine, sine)


def in_quarter(turns, cosine, sine):
    quarter = turns & 3
    odd = (quarter & 1) == 1
    c = jnp.where(odd, sine, cosine)
    s = jnp.where(odd, cosine, sine)
    c = jnp.where((quarter == 1) | (quarter == 2), -c, c)
    s = jnp.where(quarter >= 2, -s, s)
    return (c, s)


def cosine_and_sine(angle):
    scaled = angle * (2.0 / math.pi)
    turns = (scaled + jnp.where(scaled >= 0.0, 0.5, -0.5)).astype(jnp.int32)
    count = turns.astype(F32)
    x = angle - count * 1.5703125
    x = x - count * 4.837512969970703125e-4
    x = x - count * 7.5497899548918822e-8
    return in_quarter(turns, *small_cosine_and_sine(x))


def twist(number):
    turns = (number + TIME // 8) >> 14
    rest = (number - (turns << 14)).astype(F32)
    return in_quarter(turns, *small_cosine_and_sine(rest * (2.0 * math.pi / TIME)))


def row_and_lane():
    return (lax.broadcasted_iota(jnp.int32, (8, LANES), axis) for axis in range(2))


def small_kernel(th_ref, small_ref):
    row, lane = (lax.broadcasted_iota(jnp.int32, (LANES, LANES), axis) for axis in range(2))
    small_ref[0], small_ref[1] = twist(4 * row * lane)


def rotor_kernel(th_ref, tl_ref, beta_ref, after_ref, rotor_ref):
    own = lax.broadcasted_iota(jnp.int32, beta_ref.shape, 1) == th_ref[0]
    beta = jnp.sum(jnp.where(own, beta_ref[...], 0.0), axis=1, keepdims=True)
    offset, slope, curve = (beta[k : k + 1, :] for k in range(3))
    row, lane = (lax.broadcasted_iota(jnp.int32, (LANES, LANES), axis) for axis in range(2))
    wave = 4 * (row + LANES * lane) + tl_ref[0]
    signed = jnp.where(wave < TIME // 2, wave, wave - TIME)
    frequency = signed.astype(F32) * (1.0 / (TIME / 2))
    angle = (
        math.pi * offset
        + 300.0 * slope * frequency
        + 3000.0 * curve * frequency * frequency
    )
    rotor_ref[0], rotor_ref[1] = cosine_and_sine(angle)


def enter_kernel(field_ref, after_ref, out_ref):
    for ri in range(2):
        for tile in range(32):
            zb, rest = (tile // 4 % 4, tile // 16 * 4 + tile % 4)
            out_ref[pl.ds(zb * 16 + ri * 8 + rest, 4, stride=64), :] = field_ref[
                ri, :, tile * LANES : (tile + 1) * LANES
            ]


def radix_ahead(x):
    (r0, i0), (r1, i1), (r2, i2), (r3, i3) = x
    sr, si, dr, di = r0 + r2, i0 + i2, r0 - r2, i0 - i2
    tr, ti, ur, ui = r1 + r3, i1 + i3, r1 - r3, i1 - i3
    return [(sr + tr, si + ti), (dr + ui, di - ur), (sr - tr, si - ti), (dr - ui, di + ur)]


def radix_back(x):
    out = radix_ahead(x)
    return [out[0], out[3], out[2], out[1]]


def turned_back(pair, c, s):
    re, im = pair
    return (re * c + im * s, im * c - re * s)


def turned(pair, c, s):
    return turned_back(pair, c, -s)


def first_radix_kernel(zb_ref, x_ref, out_ref):
    row, lane = row_and_lane()
    place = (row // 4) * 2048 + (row % 4) * LANES + lane + zb_ref[0] * 512
    for v2 in range(4):
        at = [a * 64 + v2 * 16 for a in range(4)]
        y = radix_ahead([(x_ref[b : b + 8, :], x_ref[b + 8 : b + 16, :]) for b in at])
        for f in range(4):
            pair = turned_back(y[f], *twist(f * (place + v2 * 4096))) if f else y[f]
            for ri in range(2):
                for v0 in range(2):
                    first = BACKWARD[f] * 64 + ri * 8 + v2 * 2 + v0
                    out_ref[pl.ds(first, 4, stride=16), :] = pair[ri][v0 * 4 : v0 * 4 + 4]


def middle_twists(th_ref, tl_ref):
    row, lane = row_and_lane()
    place = row * 2048 + lane + (th_ref[0] * 4 + tl_ref[0]) * LANES
    return [None] + [twist(f * place) for f in range(1, 4)]


def ahead_kernel(th_ref, tl_ref, x_ref, out_ref):
    twists = middle_twists(th_ref, tl_ref)
    for low in range(4):
        y = radix_ahead(
            [
                tuple(x_ref[pl.ds(a * 64 + low * 2 + ri, 8, stride=8), :] for ri in range(2))
                for a in range(4)
            ]
        )
        for f in range(4):
            re, im = turned_back(y[f], *twists[f]) if f else y[f]
            at = low * 64 + f * 16
            out_ref[at : at + 8, :] = re
            out_ref[at + 8 : at + 16, :] = im


def back_kernel(th_ref, tl_ref, x_ref, out_ref):
    twists = middle_twists(th_ref, tl_ref)
    for low in range(4):
        y = []
        for f in range(4):
            at = low * 64 + f * 16
            pair = (x_ref[at : at + 8, :], x_ref[at + 8 : at + 16, :])
            y.append(turned(pair, *twists[f]) if f else pair)
        for a, pair in enumerate(radix_back(y)):
            for ri in range(2):
                out_ref[pl.ds(a * 64 + low * 2 + ri, 8, stride=8), :] = pair[ri]


def spectral_kernel(order, x_ref, rotor_ref, small_ref, waves_ref, out_ref):
    rotor = (rotor_ref[0], rotor_ref[1])
    small = (small_ref[0], small_ref[1])
    x = jnp.concatenate([x_ref[64 * k : 64 * k + 64, :] for k in order], axis=0)
    y = from_left(waves_ref, 0, x)
    re, im = turned_back((y[:LANES], y[LANES:]), *small)
    y = from_right(jnp.concatenate([re, im], axis=1), waves_ref, 1)
    re, im = turned((y[:, :LANES], y[:, LANES:]), *rotor)
    y = from_right(jnp.concatenate([re, im], axis=1), waves_ref, 2)
    re, im = turned((y[:, :LANES], y[:, LANES:]), *small)
    out_ref[...] = from_left(waves_ref, 3, jnp.concatenate([re, im], axis=0))


def one_hots(quartets_ref, modes):
    ids = lax.broadcasted_iota(jnp.int32, (modes, quartets_ref.shape[1]), 0)
    return [
        jnp.where(quartets_ref[k : k + 1, :] == ids, 1.0, 0.0).astype(BF16) for k in range(4)
    ]


def kerr_term(fields, hot, weights_ref):
    size = fields.shape[0] // 2
    parts = jnp.concatenate(split(fields), axis=1)
    total = None
    for start in range(0, weights_ref.shape[1], TILE):
        here = slice(start, start + TILE)
        (lr, li), (mr, mi), (nr, ni) = (
            (y[:size], y[size:])
            for y in (dot(parts, jnp.concatenate([hot[k][:, here]] * 2, axis=0)) for k in (1, 2, 3))
        )
        weight = weights_ref[:, here]
        pr, pi = (lr * mr - li * mi, lr * mi + li * mr)
        pr, pi = (pr * weight, pi * weight)
        terms = jnp.concatenate([pr * ni - pi * nr, pr * nr + pi * ni], axis=0)
        terms = jnp.concatenate(split(terms), axis=1)
        added = lax.dot_general(
            terms,
            jnp.concatenate([hot[0][:, here]] * 2, axis=1),
            (((1,), (1,)), ((), ())),
            preferred_element_type=F32,
        )
        total = added if total is None else total + added
    return total


def kerr_kernel(last, x_ref, quartets_ref, weights_ref, *refs):
    modes = x_ref.shape[0] // 2
    linear = jnp.concatenate(
        [x_ref[pl.ds(ri, modes, stride=2), :].T for ri in range(2)], axis=0
    )
    hot = one_hots(quartets_ref, modes)
    first = kerr_term(linear, hot, weights_ref)
    second = kerr_term(linear + first, hot, weights_ref)
    updated = linear + 0.5 * (first + second)
    estimate = 0.5 * (second - first)
    sums = [jnp.sum(y * y, axis=0, keepdims=True) for y in (estimate, updated)]
    if not last:
        out_ref, sums_ref = refs
        for ri in range(2):
            out_ref[pl.ds(ri, modes, stride=2), :] = updated[ri * LANES : (ri + 1) * LANES].T
        sums_ref[0:1, :] = sums[0]
        sums_ref[1:2, :] = sums[1]
        return
    before_ref, out_ref, held_ref = refs
    for ri in range(2):
        held_ref[pl.ds(ri, modes, stride=2), :] = updated[ri * LANES : (ri + 1) * LANES].T
    norms = [before_ref[0:1, :], before_ref[1:2, :], *sums]
    shape = (modes // 4, modes)
    own = lax.broadcasted_iota(jnp.int32, shape, 1) // 4 == lax.broadcasted_iota(jnp.int32, shape, 0)
    picked = jnp.concatenate([jnp.where(own, norm, 0.0) for norm in norms], axis=1)
    shape = (4 * modes, LANES)
    source = lax.broadcasted_iota(jnp.int32, shape, 0)
    target = source // modes * 4 + source % 4
    moves = jnp.where(lax.broadcasted_iota(jnp.int32, shape, 1) == target, 1.0, 0.0).astype(BF16)
    high, low = split(picked)
    rows = dot(high, moves) + dot(low, moves)
    for group in range(modes // 4):
        out_ref[group * 9 : group * 9 + 8, :] = held_ref[group * 8 : group * 8 + 8, :]
        out_ref[group * 9 + 8 : group * 9 + 9, :] = rows[group : group + 1, :]


def regroup_kernel(x_ref, out_ref):
    norms = x_ref[8:9, :]
    for source in range(1, 32):
        norms = norms + x_ref[source * 9 + 8 : source * 9 + 9, :]
    for target in range(16):
        for half in range(2):
            source = target * 2 + half
            at = target * 17 + half * 8
            out_ref[at : at + 8, :] = x_ref[source * 9 : source * 9 + 8, :]
        out_ref[target * 17 + 16 : target * 17 + 17, :] = norms


def leave_kernel(x_ref, field_ref, errors_ref):
    norms = x_ref[16:17, :]
    for source in range(1, 16):
        norms = norms + x_ref[source * 17 + 16 : source * 17 + 17, :]
    size = pltpu.roll(norms, LANES - 4, 1)
    ratio = jnp.sqrt(norms / (size + EPSILON))
    errors_ref[0:1, :] = ratio[:, 0:4]
    errors_ref[1:2, :] = ratio[:, 8:12]
    for source in range(16):
        for half in range(2):
            tile = half * 16 + source
            for ri in range(2):
                field_ref[ri, :, tile * LANES : (tile + 1) * LANES] = x_ref[
                    pl.ds(source * 17 + half * 8 + ri, 4, stride=2), :
                ]


def rows_of(count):
    return jax.ShapeDtypeStruct((count, LANES), F32)


def exchange(array, axes, peers):
    rows = array.shape[0] // peers
    tile = 1
    tiles = array.reshape(peers, rows // tile, tile, LANES)
    return lax.all_to_all(tiles, axes, 0, 0, tiled=True).reshape(array.shape)


def shards(field, beta, quartets, intersections):
    waves = jnp.asarray(host_waves())
    th, tl = (lax.axis_index(a).astype(jnp.int32)[None] for a in ("th", ("t1", "t0")))
    weights = intersections.reshape(1, -1)
    along, across = (("th", "t1", "t0"), "mode")
    vmem = pl.BlockSpec(memory_space=pltpu.VMEM)
    smem = pl.BlockSpec(memory_space=pltpu.SMEM)
    limit = pltpu.CompilerParams(vmem_limit_bytes=16 * 1024 * 1024)

    def placed(kernel, state, *numbers):
        return pl.pallas_call(
            kernel,
            out_shape=rows_of(256),
            in_specs=[smem] * len(numbers) + [vmem],
            out_specs=vmem,
            compiler_params=limit,
        )(*numbers, state)

    def spectral(state, order):
        return pl.pallas_call(
            functools.partial(spectral_kernel, order),
            out_shape=rows_of(256),
            in_specs=[vmem] * 4,
            out_specs=vmem,
            compiler_params=limit,
        )(state, rotor, small, waves)

    square = jax.ShapeDtypeStruct((2, LANES, LANES), F32)
    small = pl.pallas_call(
        small_kernel,
        out_shape=square,
        in_specs=[smem],
        out_specs=vmem,
        compiler_params=limit,
        cost_estimate=pl.CostEstimate(flops=10**9, bytes_accessed=2 * TIME, transcendentals=0),
    )(th)
    rotor = pl.pallas_call(
        rotor_kernel,
        out_shape=square,
        in_specs=[smem] * 2 + [vmem] * 2,
        out_specs=vmem,
        compiler_params=limit,
        cost_estimate=pl.CostEstimate(flops=10**8, bytes_accessed=2 * TIME, transcendentals=0),
    )(th, tl, beta, small)
    state = pl.pallas_call(
        enter_kernel,
        out_shape=rows_of(256),
        in_specs=[vmem, vmem],
        out_specs=vmem,
        compiler_params=limit,
    )(field, rotor)
    state = exchange(state, along, 16)
    state = placed(first_radix_kernel, state, tl)
    state = exchange(state, ("t0", "t1"), 4)
    norms = []
    for step in range(STEPS):
        last = step == STEPS - 1
        state = spectral(state, range(4) if step else BACKWARD)
        state = exchange(state, along, 16)
        state = placed(back_kernel, state, th, tl)
        state = exchange(state, across, 32)
        out = pl.pallas_call(
            functools.partial(kerr_kernel, last),
            out_shape=rows_of(288) if last else (rows_of(256), rows_of(8)),
            in_specs=[vmem] * (3 + len(norms)),
            out_specs=vmem if last else (vmem, vmem),
            scratch_shapes=[pltpu.VMEM((256, LANES), F32)] if last else [],
            compiler_params=limit,
        )(state, quartets, weights, *norms)
        if last:
            state = exchange(out, across, 32)
            break
        state, norm = out
        norms.append(norm)
        state = exchange(state, across, 32)
        state = placed(ahead_kernel, state, th, tl)
        state = exchange(state, along, 16)
    state = pl.pallas_call(
        regroup_kernel,
        out_shape=rows_of(272),
        in_specs=[vmem],
        out_specs=vmem,
        compiler_params=limit,
    )(state)
    state = exchange(state, along, 16)
    return pl.pallas_call(
        leave_kernel,
        out_shape=(
            jax.ShapeDtypeStruct(field.shape, F32),
            jax.ShapeDtypeStruct((STEPS, field.shape[1]), F32),
        ),
        in_specs=[vmem],
        out_specs=(vmem, vmem),
        compiler_params=limit,
    )(state)


def solution(mesh):
    finer = Mesh(mesh.devices.reshape(-1, 4, 2, 2), ("mode", "th", "t1", "t0"))
    times = ("th", "t1", "t0")
    return jax.shard_map(
        shards,
        mesh=finer,
        in_specs=(P(None, "mode", times), P(None, "mode"), P(), P()),
        out_specs=(P(None, "mode", times), P(None, "mode")),
        check_vma=False,
    )
```
